512 devices in a mesh: batch: 8 (over z), pos: 64 (over y, x, core).
Axes of the slice: x: 4, y: 8, z: 8, core: 2. Of those that a mesh axis runs over, the one named last changes fastest.
Arguments:
- cand_proj: bfloat16 [8192, 4096], P(('batch', 'pos')), may hold values from -6 to 6
- cand_input: bfloat16 [8192, 1024], P(('batch', 'pos')), may hold values from -6 to 6
- kv_pool: bfloat16 [64, 2, 2048, 1024], P('batch', None, 'pos'), may hold values from -6 to 6
- page_owner: int32 [8, 64, 8], P('batch', 'pos'), may hold values from 0 to 7, as said below
- page_slot: int32 [8, 64, 8], P('batch', 'pos'), may hold values from 0 to 7, as said below
- lengths: int32 [8], P('batch'), may hold values from 4096 to 16384
- block_mask: int32 [8, 8, 128], P('batch', None, 'pos'), may hold values 0 or 1
- out_gain: float32 [1024], replicated, may hold values from 0.5 to 1.5
- out_weight: bfloat16 [1024, 1024], replicated, may hold values from -0.1875 to 0.1875
Outputs:
- cand_output: bfloat16 [8192, 1024], P(('batch', 'pos'))
The draws below stay inside these ranges and needn't reach their ends.
Inputs may be any that keep to these rules, and one draw needn't show every extreme that they name: `page_owner`: for each user and each index of pos, every index of batch appears exactly 1 times among the 8 pages. At one index of pos, the pairs (page_owner, page_slot) of all users are distinct.
All inputs are finite; a program needn't handle non-finite values. No bound on the sum of `block_mask` on one device may be relied on, other than what follows from the above.
Results may differ from the reference program's by a relative error of at most 0.0095.
Values may be sent and summed in bfloat16 or wider, within the bound.
No kernel may reach another device: no remote copies, remote signals or barrier semaphores. Data moves between devices by JAX's collectives and lax.ppermute only.
A program may use at most 128 MiB of HBM per device.

```python
import jax
import jax.numpy as jnp
from jax import lax

D = 1024
HEADS = 8
C = 1024
PAGE = 32
TILE = 128
PMAX = 8
USERS = 8
SLOTS = 8
CAP = 1
HIST = 16384
CANDS = 8192
CTILES = 8
HTILES = 128
N_BATCH = 8
N_POS = 64


def page_table(key):
    count = N_BATCH * N_POS
    first = jax.random.split(jax.random.fold_in(key, 11), count)
    second = jax.random.split(jax.random.fold_in(key, 12), count)
    order = jax.vmap(lambda part_key: jax.random.permutation(part_key, PMAX))(first).reshape(N_BATCH, N_POS, PMAX)
    places = jax.vmap(lambda part_key: jax.random.permutation(part_key, SLOTS))(second).reshape(N_BATCH, N_POS, SLOTS)
    owner = order // CAP
    within = order % CAP
    requester = jnp.arange(N_BATCH, dtype=jnp.int32)[:, None, None]
    column = jnp.arange(N_POS, dtype=jnp.int32)[None, :, None]
    slot = places[owner, column, requester * CAP + within]
    return (owner.astype(jnp.int32), slot.astype(jnp.int32))


def draw_page_owner(key, part):
    owner, slot = page_table(key)
    return owner


def draw_page_slot(key, part):
    owner, slot = page_table(key)
    return slot


def place_ends(array, own_key, least, top_value):
    extent = array.shape
    index_at = [jax.random.randint(jax.random.fold_in(own_key, axis), (), 0, extent[axis]) for axis in range(len(extent))]
    array = array.at[tuple(index_at)].set(least)
    longest = extent.index(max(extent))
    index_at[longest] = (index_at[longest] + 1) % extent[longest]
    return array.at[tuple(index_at)].set(top_value)


def block_scale(rng, shape, pieces, least, high):
    factor_of, own = 1.0, jax.random.fold_in(rng, 6)
    for dim, shards_of in pieces:
        draws = jnp.exp(jax.random.uniform(jax.random.fold_in(own, dim), (shards_of,), jnp.float32, least / len(pieces), high / len(pieces)))
        factor_of = factor_of * jnp.repeat(draws, shape[dim] // shards_of).reshape([-1 if axis == dim else 1 for axis in range(len(shape))])
    return factor_of


def centred(key, dims, scale, bound, cuts=(), kind=jnp.bfloat16):
    loudness = block_scale(key, dims, cuts, -0.22, 0.18) if cuts else 1.0
    values = jax.random.normal(key, dims, jnp.float32) * scale * loudness
    return jnp.minimum(jnp.maximum(values, -bound), bound).astype(kind)


def setup_inputs(seed: int = 0) -> dict:
    key_of = jax.random.split(jax.random.key(seed), 10)
    cand_proj = centred(key_of[0], (CANDS, 4 * D), 1.0, 6.0, ((0, 512),))
    cand_input = centred(key_of[1], (CANDS, D), 1.0, 6.0, ((0, 512),))
    kv_pool = centred(key_of[2], (N_BATCH * SLOTS, 2, N_POS * PAGE, D), 1.0, 6.0, ((0, 8), (2, 64)))
    page_owner = draw_page_owner(jax.random.fold_in(key_of[9], 71), 0)
    page_slot = draw_page_slot(jax.random.fold_in(key_of[9], 71), 0)
    lengths = place_ends(jax.random.randint(key_of[5], (USERS,), HIST // 4, HIST + 1), jax.random.fold_in(key_of[5], 1), HIST // 4, HIST).astype(jnp.int32)
    block_mask = place_ends((jax.random.randint(key_of[6], (USERS, CTILES, HTILES), 0, 4) < 3).astype(jnp.int32), jax.random.fold_in(key_of[6], 1), 0, 1)
    out_gain = jnp.clip(1.0 + 0.1 * jax.random.normal(key_of[7], (D,), jnp.float32), 0.5, 1.5)
    out_weight = centred(key_of[8], (D, D), D ** -0.5, 0.1875)
    return dict(cand_proj=cand_proj, cand_input=cand_input, kv_pool=kv_pool, page_owner=page_owner, page_slot=page_slot, lengths=lengths, block_mask=block_mask, out_gain=out_gain, out_weight=out_weight)


eps = 1e-05

def reference(cand_proj, cand_input, kv_pool, page_owner, page_slot, lengths, block_mask, out_gain, out_weight):
    width = cand_input.shape[1]
    headsize = width // HEADS
    scale = headsize ** (-0.5)
    pool = kv_pool.reshape(N_BATCH, SLOTS, 2, N_POS, PAGE, width)
    column = jnp.arange(N_POS, dtype=jnp.int32)[:, None]
    projections = cand_proj.reshape(USERS, C, 4 * width)
    inputs = cand_input.reshape(USERS, C, width)
    tile_of_row = jnp.arange(C, dtype=jnp.int32) // TILE

    def one_user(packed):
        proj, owner, slot, length, mask, layer_in = packed
        act = jax.nn.silu(proj.astype(jnp.float32)).astype(jnp.bfloat16)
        u_act = act[:, :width]
        v_act = act[:, width:2 * width]
        q_act = act[:, 2 * width:3 * width]
        k_act = act[:, 3 * width:]
        got = pool[owner, slot, :, column, :, :]
        hist = jnp.transpose(got, (2, 0, 1, 3, 4)).reshape(2, HIST, width)
        query = q_act.astype(jnp.float32).reshape(C, HEADS, headsize)

        def step(total, index):
            start = (index * TILE).astype(jnp.int32)
            keys = lax.dynamic_slice_in_dim(hist[0], start, TILE, 0).astype(jnp.float32).reshape(TILE, HEADS, headsize)
            values = lax.dynamic_slice_in_dim(hist[1], start, TILE, 0).astype(jnp.float32).reshape(TILE, HEADS, headsize)
            where = start + jnp.arange(TILE, dtype=jnp.int32)
            block = lax.dynamic_index_in_dim(mask, index, 1, keepdims=False)[tile_of_row]
            allowed = (block[:, None] == 1) & (where[None, :] < length)
            scores = jnp.einsum('rhd,thd->hrt', query, keys) * scale
            weight = jnp.where(allowed[None], jax.nn.silu(scores), 0.0).astype(jnp.bfloat16)
            total = total + jnp.einsum('hrt,thd->rhd', weight.astype(jnp.float32), values)
            return (total, None)
        total, _ = lax.scan(step, jnp.zeros((C, HEADS, headsize), jnp.float32), jnp.arange(HTILES, dtype=jnp.int32))
        key_own = k_act.astype(jnp.float32).reshape(C, HEADS, headsize)
        own = jax.nn.silu(lax.optimization_barrier(jnp.sum(query * key_own, axis=-1)) * scale).astype(jnp.bfloat16)
        total = total + own.astype(jnp.float32)[:, :, None] * v_act.astype(jnp.float32).reshape(C, HEADS, headsize)
        attn = total.reshape(C, width)
        mean = lax.optimization_barrier(jnp.mean(attn, axis=-1, keepdims=True))
        centered = attn - mean
        var = lax.optimization_barrier(jnp.mean(centered * centered, axis=-1, keepdims=True))
        normed = (centered * lax.rsqrt(var + eps) * out_gain.astype(jnp.float32) * u_act.astype(jnp.float32)).astype(jnp.bfloat16)
        result = layer_in.astype(jnp.float32) + jnp.dot(normed, out_weight, preferred_element_type=jnp.float32)
        return result.astype(jnp.bfloat16)
    outputs = lax.map(one_user, (projections, page_owner, page_slot, lengths, block_mask, inputs))
    return outputs.reshape(CANDS, width)
```

```python
import functools

import jax
import jax.numpy as jnp
from jax import lax
from jax.experimental import pallas as pl
from jax.experimental.pallas import tpu as pltpu
from jax.sharding import Mesh
from jax.sharding import PartitionSpec as P

HEADS = 8
PAGE = 32
eps = 1e-05

PLANE = ("y", "x", "c")
SPREAD = ("z", "x", "c")


def exchange(array, axes):
    return lax.all_to_all(array, axes, split_axis=0, concat_axis=0, tiled=True)


def split_pages_kernel(slot_ref, page_ref, out_ref):
    hd = out_ref.shape[2]
    for h in range(HEADS):
        for kv in range(2):
            out_ref[h, kv * PAGE : (kv + 1) * PAGE, :] = page_ref[0, kv, :, h * hd : (h + 1) * hd]


def split_pages(slots, kv_pool):
    count, _, page, width = kv_pool.shape
    users = slots.shape[0]
    hd = width // HEADS
    return pl.pallas_call(
        split_pages_kernel,
        grid_spec=pltpu.PrefetchScalarGridSpec(
            num_scalar_prefetch=1,
            grid=(users,),
            in_specs=[pl.BlockSpec((1, 2, page, width), lambda u, slot: (slot[u], 0, 0, 0))],
            out_specs=pl.BlockSpec((HEADS, 2 * page, hd), lambda u, slot: (u, 0, 0)),
        ),
        out_shape=jax.ShapeDtypeStruct((users * HEADS, 2 * page, hd), kv_pool.dtype),
        name="split_pages",
    )(slots, kv_pool)


def attend_kernel(scale, q_ref, kv_ref, mask_ref, out_ref, acc_ref):
    rows, hd = q_ref.shape
    pages = kv_ref.shape[0]
    step = 8
    span = step * PAGE
    tiles = mask_ref.shape[0]
    q = q_ref[...]
    for i in range(pages // step):
        block = kv_ref[i * step : (i + 1) * step]
        keys = block[:, :PAGE, :].reshape(span, hd)
        values = block[:, PAGE:, :].reshape(span, hd)
        half = lax.dot_general(q, keys, (((1,), (1,)), ((), ())), preferred_element_type=jnp.float32)
        half = half * (0.5 * scale)
        weight = (half + half * jnp.tanh(half)).astype(jnp.bfloat16)
        allowed = mask_ref[:, i * span : (i + 1) * span]
        weight = weight.reshape(tiles, rows // tiles, span) * allowed[:, None, :]
        part = jnp.dot(weight.reshape(rows, span), values, preferred_element_type=jnp.float32)
        if i == 0:
            acc_ref[...] = part
        else:
            acc_ref[...] += part
    out_ref[...] = acc_ref[...].astype(out_ref.dtype)


def attend(query, pages, mask, scale):
    rows, hd = query.shape
    return pl.pallas_call(
        functools.partial(attend_kernel, scale),
        in_specs=[pl.BlockSpec(memory_space=pltpu.VMEM)] * 3,
        out_specs=pl.BlockSpec(memory_space=pltpu.VMEM),
        out_shape=jax.ShapeDtypeStruct((rows, hd), jnp.bfloat16),
        scratch_shapes=[pltpu.VMEM((rows, hd), jnp.float32)],
        compiler_params=pltpu.CompilerParams(vmem_limit_bytes=40 * 1024 * 1024),
        name="attend",
    )(query, pages, mask)


def on_device(
    cand_proj, cand_input, kv_pool, page_owner, page_slot, lengths, block_mask, out_gain, out_weight
):
    rows, width = cand_input.shape
    hd = width // HEADS
    scale = hd ** (-0.5)
    n_z, n_y = lax.axis_size("z"), lax.axis_size("y")
    n_h = lax.axis_size("x") * lax.axis_size("c")
    me_z = lax.axis_index("z")
    me_h = lax.axis_index(("x", "c"))
    position = lax.axis_index(PLANE)

    owners, slots = page_owner.reshape(-1), page_slot.reshape(-1)
    pages = owners.shape[0]
    hit = (owners[None, :] == jnp.arange(n_z, dtype=jnp.int32)[:, None]).astype(jnp.int32)
    index = jnp.arange(pages, dtype=jnp.int32)
    slot_of = jnp.sum(hit * slots[None, :], axis=1)
    live = jnp.clip(lengths[0] - (position * pages + index) * PAGE, 0, PAGE)
    live_of = jnp.sum(hit * live[None, :], axis=1)
    seen = jnp.repeat(block_mask[0], pages // block_mask.shape[2], axis=1)
    seen_of = jnp.sum(hit[:, None, :] * seen[None, :, :], axis=2)
    tiles = seen.shape[0]
    info = jnp.concatenate([slot_of[:, None], live_of[:, None], seen_of], axis=1).reshape(-1)
    info = jnp.pad(info, (0, 128 - info.shape[0]))
    told = exchange(jnp.broadcast_to(info[None], (n_z * n_h, 128)), SPREAD)
    told = told[:, : n_z * (tiles + 2)].reshape(n_z, n_h, n_z, tiles + 2)
    served = lax.dynamic_index_in_dim(told[:, :, :, 0], me_h, 1, keepdims=False)
    served = lax.dynamic_index_in_dim(served, me_z, 1, keepdims=False)
    mine = lax.dynamic_index_in_dim(told, me_z, 0, keepdims=False)
    mine = mine.transpose(2, 1, 0)
    alive = jnp.arange(PAGE, dtype=jnp.int32) < mine[1][:, :, None]
    mask = (mine[2:, :, :, None] == 1) & alive[None]
    mask = mask.reshape(tiles, -1).astype(jnp.bfloat16)

    act = jax.nn.silu(cand_proj.astype(jnp.float32)).astype(jnp.bfloat16)
    u_act = act[:, :width]
    v_act = act[:, width : 2 * width]
    q_act = act[:, 2 * width : 3 * width]
    k_act = act[:, 3 * width :]
    by_head = q_act.reshape(rows, HEADS, hd).transpose(1, 0, 2)
    sent = jnp.broadcast_to(by_head[None], (n_y, HEADS, rows, hd)).reshape(n_y * HEADS, rows, hd)
    query = exchange(sent, PLANE).reshape(-1, hd)

    got = exchange(split_pages(served, kv_pool), SPREAD)
    part = attend(query, got, mask, scale)
    back = exchange(part.reshape(n_y * n_h, rows, hd), PLANE)
    attn = jnp.sum(back.reshape(n_y, HEADS, rows, hd).astype(jnp.float32), axis=0)
    attn = attn.transpose(1, 0, 2)

    query_own = q_act.astype(jnp.float32).reshape(rows, HEADS, hd)
    key_own = k_act.astype(jnp.float32).reshape(rows, HEADS, hd)
    own = jax.nn.silu(jnp.sum(query_own * key_own, axis=-1) * scale).astype(jnp.bfloat16)
    attn = attn + own.astype(jnp.float32)[:, :, None] * v_act.astype(jnp.float32).reshape(
        rows, HEADS, hd
    )
    attn = attn.reshape(rows, width)
    mean = jnp.mean(attn, axis=-1, keepdims=True)
    centered = attn - mean
    var = jnp.mean(centered * centered, axis=-1, keepdims=True)
    normed = (centered * lax.rsqrt(var + eps) * out_gain * u_act.astype(jnp.float32)).astype(
        jnp.bfloat16
    )
    result = cand_input.astype(jnp.float32) + jnp.dot(
        normed, out_weight, preferred_element_type=jnp.float32
    )
    return result.astype(jnp.bfloat16)


def solution(mesh):
    n_z, n_p = mesh.shape["batch"], mesh.shape["pos"]
    cores, n_x = 2, HEADS // 2
    grid = Mesh(mesh.devices.reshape(n_z, n_p // HEADS, n_x, cores), ("z", "y", "x", "c"))
    rows = P(("z", "y", "x", "c"), None)
    placed = (
        rows,
        rows,
        P("z", None, PLANE, None),
        P("z", PLANE, None),
        P("z", PLANE, None),
        P("z"),
        P("z", None, PLANE),
        P(),
        P(),
    )
    return jax.shard_map(on_device, mesh=grid, in_specs=placed, out_specs=rows, check_vma=False)
```

```python
import functools

import jax
import jax.numpy as jnp
from jax import lax
from jax.experimental import pallas as pl
from jax.experimental.pallas import tpu as pltpu
from jax.sharding import Mesh
from jax.sharding import PartitionSpec as P

HEADS = 8
PAGE = 32
eps = 1e-05

PLANE = ("y", "x", "c")
SPREAD = ("z", "x", "c")

FIELDS = 16
LIVE, SLOT = 8, 9

VMEM = pl.BlockSpec(memory_space=pltpu.VMEM)
SMEM = pl.BlockSpec(memory_space=pltpu.SMEM)
HBM = pl.BlockSpec(memory_space=pl.ANY)


def exchange(array, axes):
    return lax.all_to_all(array, axes, split_axis=0, concat_axis=0, tiled=True)


def shift(array, axis, step):
    n = lax.axis_size(axis)
    return lax.ppermute(array, axis, [(i, (i + step) % n) for i in range(n)])


def silu(value):
    half = value * 0.5
    return half + half * jnp.tanh(half)


def announce_kernel(place_ref, owner_ref, slot_ref, length_ref, seen_ref, q_ref, out_ref):
    rows = q_ref.shape[0]
    pages = owner_ref.shape[0]
    tiles, blocks = seen_ref.shape
    hd = out_ref.shape[2]
    lane = lax.broadcasted_iota(jnp.int32, (8, hd), 1)
    owner, field = lane // FIELDS, lane % FIELDS
    seen = []
    for b in range(blocks):
        row = jnp.zeros((8, hd), jnp.int32)
        for t in range(tiles):
            row = jnp.where(field == t, seen_ref[t, b], row)
        seen.append(row)
    info = jnp.zeros((8, hd), jnp.int32)
    for j in range(pages):
        live = jnp.clip(length_ref[0] - (place_ref[0] * pages + j) * PAGE, 0, PAGE)
        row = jnp.where(field == LIVE, live, seen[j * blocks // pages])
        row = jnp.where(field == SLOT, slot_ref[j], row)
        info = jnp.where(owner == owner_ref[j], row, info)
    info = info.astype(jnp.float32).astype(jnp.bfloat16)
    query = silu(q_ref[...].astype(jnp.float32)).astype(jnp.bfloat16)
    for h in range(HEADS):
        chunk = jnp.concatenate([query[:, h * hd : (h + 1) * hd], info], axis=0)
        for z in range(out_ref.shape[0] // HEADS):
            out_ref[z * HEADS + h] = chunk


def announce(place, owners, slots, lengths, seen, cand_proj, users):
    rows, width = cand_proj.shape[0], cand_proj.shape[1] // 4
    hd = width // HEADS
    return pl.pallas_call(
        announce_kernel,
        grid=(1,),
        in_specs=[SMEM] * 5 + [pl.BlockSpec((rows, width), lambda i: (0, 2))],
        out_specs=VMEM,
        out_shape=jax.ShapeDtypeStruct((users * HEADS, rows + 8, hd), jnp.bfloat16),
        name="announce",
    )(place, owners, slots, lengths, seen, cand_proj)


def split_pages_kernel(slot_ref, pool_ref, out_ref, sems):
    hd = out_ref.shape[3]
    copies = []
    for u in range(slot_ref.shape[0]):
        for h in range(HEADS):
            copies.append(
                pltpu.make_async_copy(
                    pool_ref.at[slot_ref[u], :, :, pl.ds(h * hd, hd)],
                    out_ref.at[u * HEADS + h],
                    sems.at[u * HEADS + h],
                )
            )
    for copy in copies:
        copy.start()
    for copy in copies:
        copy.wait()


def split_pages(slots, kv_pool):
    _, _, page, width = kv_pool.shape
    users = slots.shape[0]
    return pl.pallas_call(
        split_pages_kernel,
        in_specs=[SMEM, HBM],
        out_specs=HBM,
        out_shape=jax.ShapeDtypeStruct((users * HEADS, 2, page, width // HEADS), kv_pool.dtype),
        scratch_shapes=[pltpu.SemaphoreType.DMA((users * HEADS,))],
        name="split_pages",
    )(slots, kv_pool)


STEPS = (0, -1, 1, -3, -4, -2, 3, 2)


def gather_queries(row):
    below, above = shift(row, "y", 1), shift(row, "y", -1)
    below3 = shift(jnp.concatenate([row, below, above]), "y", 3)
    above3 = shift(jnp.concatenate([row, below]), "y", -3)
    return row, below, above, below3, above3


def attend_kernel(scale, y_ref, info_ref, kv_ref, *rest):
    pieces, (out_ref, q_ref, acc_ref) = rest[:-3], rest[-3:]
    hd = out_ref.shape[1]
    sources, tiles = info_ref.shape[0], len(STEPS)
    span = sources * PAGE
    height = out_ref.shape[0] // tiles
    y = y_ref[0]
    place = 0
    for piece in pieces:
        for b in range(piece.shape[0] // height):
            to = lax.rem(y + (STEPS[place] + tiles), tiles)
            q_ref[pl.ds(to * height, height), :] = piece[b * height : (b + 1) * height, :]
            place += 1
    place = lax.broadcasted_iota(jnp.int32, (sources, span), 1)
    which = lax.broadcasted_iota(jnp.int32, (sources, span), 0)
    spread = (place // PAGE == which).astype(jnp.bfloat16)
    fields = lax.dot_general(
        info_ref[...], spread, (((0,), (0,)), ((), ())), preferred_element_type=jnp.float32
    )
    within = lax.rem(lax.broadcasted_iota(jnp.int32, (1, span), 1), PAGE).astype(jnp.float32)
    q = q_ref[...]
    for o in range(kv_ref.shape[0] // sources):
        keys = kv_ref[o * sources : (o + 1) * sources, 0].reshape(span, hd)
        values = kv_ref[o * sources : (o + 1) * sources, 1].reshape(span, hd)
        seen = fields[o * FIELDS : o * FIELDS + tiles]
        live = fields[o * FIELDS + LIVE : o * FIELDS + LIVE + 1]
        allowed = jnp.where(within < live, seen, 0.0).astype(jnp.bfloat16)
        score = lax.dot_general(q, keys, (((1,), (1,)), ((), ())), preferred_element_type=jnp.float32)
        weight = silu(score * scale).astype(jnp.bfloat16)
        weight = weight.reshape(tiles, height, span) * allowed[:, None, :]
        part = jnp.dot(weight.reshape(tiles * height, span), values, preferred_element_type=jnp.float32)
        if o == 0:
            acc_ref[...] = part
        else:
            acc_ref[...] += part
    out_ref[...] = acc_ref[...].astype(out_ref.dtype)


def attend(y, info, pages, pieces, scale):
    rows, hd = sum(piece.shape[0] for piece in pieces), pages.shape[-1]
    return pl.pallas_call(
        functools.partial(attend_kernel, scale),
        in_specs=[SMEM] + [VMEM] * (2 + len(pieces)),
        out_specs=VMEM,
        out_shape=jax.ShapeDtypeStruct((rows, hd), jnp.bfloat16),
        scratch_shapes=[pltpu.VMEM((rows, hd), jnp.bfloat16), pltpu.VMEM((rows, hd), jnp.float32)],
        compiler_params=pltpu.CompilerParams(vmem_limit_bytes=40 * 1024 * 1024),
        name="attend",
    )(y, info, pages, *pieces)


def finish_kernel(scale, back_ref, proj_ref, input_ref, gain_ref, weight_ref, out_ref):
    rows, width = input_ref.shape
    hd = width // HEADS

    def act(block, h):
        start = block * width + h * hd
        value = silu(proj_ref[:, start : start + hd].astype(jnp.float32))
        return value.astype(jnp.bfloat16).astype(jnp.float32)

    attn = []
    for h in range(HEADS):
        total = jnp.zeros((rows, hd), jnp.float32)
        for g in range(back_ref.shape[0] // HEADS):
            total += back_ref[g * HEADS + h].astype(jnp.float32)
        own = silu(jnp.sum(act(2, h) * act(3, h), axis=1, keepdims=True) * scale)
        own = own.astype(jnp.bfloat16).astype(jnp.float32)
        attn.append(total + own * act(1, h))
    attn = jnp.concatenate(attn, axis=1)
    mean = jnp.mean(attn, axis=1, keepdims=True)
    centered = attn - mean
    var = jnp.mean(centered * centered, axis=1, keepdims=True)
    u_act = jnp.concatenate([act(0, h) for h in range(HEADS)], axis=1)
    normed = (centered * lax.rsqrt(var + eps) * gain_ref[...] * u_act).astype(jnp.bfloat16)
    out = jnp.dot(normed, weight_ref[...], preferred_element_type=jnp.float32)
    out_ref[...] = (input_ref[...].astype(jnp.float32) + out).astype(out_ref.dtype)


def finish(back, cand_proj, cand_input, out_gain, out_weight, scale):
    return pl.pallas_call(
        functools.partial(finish_kernel, scale),
        in_specs=[VMEM] * 5,
        out_specs=VMEM,
        out_shape=jax.ShapeDtypeStruct(cand_input.shape, cand_input.dtype),
        compiler_params=pltpu.CompilerParams(vmem_limit_bytes=40 * 1024 * 1024),
        name="finish",
    )(back, cand_proj, cand_input, out_gain.reshape(1, -1), out_weight)


def on_device(
    cand_proj, cand_input, kv_pool, page_owner, page_slot, lengths, block_mask, out_gain, out_weight
):
    rows, width = cand_input.shape
    hd = width // HEADS
    scale = hd ** (-0.5)
    n_z = lax.axis_size("z")
    z, y, h = lax.axis_index("z"), lax.axis_index("y"), lax.axis_index(("x", "c"))
    place = lax.axis_index(PLANE)

    sent = announce(
        place.reshape(1), page_owner.reshape(-1), page_slot.reshape(-1), lengths, block_mask[0], cand_proj, n_z
    )
    told = exchange(sent, SPREAD).reshape(n_z, HEADS, rows + 8, hd)
    to_me = lax.dynamic_slice(told, (0, h, rows, z * FIELDS + SLOT), (n_z, 1, 1, 1)).reshape(-1)
    slots = jnp.clip(to_me.astype(jnp.int32), 0, kv_pool.shape[0] - 1)
    pages = split_pages(slots, kv_pool)
    pages, told = lax.optimization_barrier((pages, told))
    got = exchange(pages, SPREAD)
    mine = lax.dynamic_index_in_dim(told, z, 0, keepdims=False)
    pieces = gather_queries(mine[:, :rows].reshape(-1, hd))
    part = attend(y.reshape(1), mine[:, rows], got, pieces, scale)
    back = exchange(part.reshape(-1, rows, hd), PLANE)
    return finish(back, cand_proj, cand_input, out_gain, out_weight, scale)


def solution(mesh):
    n_z, n_p = mesh.shape["batch"], mesh.shape["pos"]
    cores, n_x = 2, HEADS // 2
    grid = Mesh(mesh.devices.reshape(n_z, n_p // HEADS, n_x, cores), ("z", "y", "x", "c"))
    rows = P(("z", "y", "x", "c"), None)
    placed = (
        rows,
        rows,
        P("z", None, PLANE, None),
        P("z", PLANE, None),
        P("z", PLANE, None),
        P("z"),
        P("z", None, PLANE),
        P(),
        P(),
    )
    return jax.shard_map(on_device, mesh=grid, in_specs=placed, out_specs=rows, check_vma=False)
```

```python
import functools

import jax
import jax.numpy as jnp
from jax import lax
from jax.experimental import pallas as pl
from jax.experimental.pallas import tpu as pltpu
from jax.sharding import Mesh
from jax.sharding import PartitionSpec as P

HEADS = 8
PAGE = 32
eps = 1e-05

PLANE = ("y", "x", "c")
SPREAD = ("z", "x", "c")

FIELDS = 16
LIVE, SLOT = 8, 9

VMEM = pl.BlockSpec(memory_space=pltpu.VMEM)
SMEM = pl.BlockSpec(memory_space=pltpu.SMEM)
HBM = pl.BlockSpec(memory_space=pl.ANY)


def exchange(array, axes):
    return lax.all_to_all(array, axes, split_axis=0, concat_axis=0, tiled=True)


def shift(array, axis, step):
    n = lax.axis_size(axis)
    return lax.ppermute(array, axis, [(i, (i + step) % n) for i in range(n)])


def silu(value):
    half = value * 0.5
    return half + half * jnp.tanh(half)


def announce_kernel(place_ref, owner_ref, slot_ref, length_ref, seen_ref, q_ref, out_ref):
    rows, hd = out_ref.shape[1:]
    pages = owner_ref.shape[0]
    tiles, blocks = seen_ref.shape
    lane = lax.broadcasted_iota(jnp.int32, (rows, hd), 1)
    owner, field = lane // FIELDS, lane % FIELDS
    seen = []
    for b in range(blocks):
        row = jnp.zeros((rows, hd), jnp.int32)
        for t in range(tiles):
            row = jnp.where(field == t, seen_ref[t : t + 1, b : b + 1], row)
        seen.append(row)
    info = jnp.zeros((rows, hd), jnp.int32)
    for j in range(pages):
        live = jnp.clip(length_ref[0] - (place_ref[1] * pages + j) * PAGE, 0, PAGE)
        row = jnp.where(field == LIVE, live, seen[j * blocks // pages])
        row = jnp.where(field == SLOT, slot_ref[j], row)
        info = jnp.where(owner == owner_ref[j], row, info)
    info = info.astype(jnp.float32).astype(jnp.bfloat16)
    for i in range(out_ref.shape[0]):
        out_ref[i] = info
    query = silu(q_ref[...].astype(jnp.float32)).astype(jnp.bfloat16)
    for h in range(HEADS):
        out_ref[place_ref[0] * HEADS + h] = query[:, h * hd : (h + 1) * hd]


def announce(place, owners, slots, lengths, seen, cand_proj, users):
    rows, width = cand_proj.shape[0], cand_proj.shape[1] // 4
    hd = width // HEADS
    return pl.pallas_call(
        announce_kernel,
        grid=(1,),
        in_specs=[SMEM] * 4 + [VMEM, pl.BlockSpec((rows, width), lambda i: (0, 2))],
        out_specs=VMEM,
        out_shape=jax.ShapeDtypeStruct((users * HEADS, rows, hd), jnp.bfloat16),
        name="announce",
    )(place, owners, slots, lengths, seen, cand_proj)


def split_pages_kernel(slot_ref, pool_ref, out_ref, split_ref, sems):
    hd = out_ref.shape[3]
    copies = []
    for u in range(slot_ref.shape[0]):
        for h in range(HEADS):
            split_ref[u * HEADS + h] = pool_ref[slot_ref[u], :, :, h * hd : (h + 1) * hd]
        part = pl.ds(u * HEADS, HEADS)
        copies.append(pltpu.make_async_copy(split_ref.at[part], out_ref.at[part], sems.at[u]))
        copies[-1].start()
    for copy in copies:
        copy.wait()


def split_pages(slots, kv_pool):
    _, _, page, width = kv_pool.shape
    users = slots.shape[0]
    out = jax.ShapeDtypeStruct((users * HEADS, 2, page, width // HEADS), kv_pool.dtype)
    return pl.pallas_call(
        split_pages_kernel,
        in_specs=[SMEM, VMEM],
        out_specs=HBM,
        out_shape=out,
        scratch_shapes=[pltpu.VMEM(out.shape, out.dtype), pltpu.SemaphoreType.DMA((users,))],
        name="split_pages",
    )(slots, kv_pool)


STEPS = (0, -1, 1, -3, -4, -2, 3, 2)


def gather_queries(row):
    below, above = shift(row, "y", 1), shift(row, "y", -1)
    below3 = shift(jnp.concatenate([row, below, above]), "y", 3)
    above3 = shift(jnp.concatenate([row, below]), "y", -3)
    return row, below, above, below3, above3


def attend_kernel(scale, y_ref, info_ref, kv_ref, *rest):
    pieces, (out_ref, q_ref, acc_ref) = rest[:-3], rest[-3:]
    hd = out_ref.shape[1]
    sources, tiles = info_ref.shape[0], len(STEPS)
    span = sources * PAGE
    height = out_ref.shape[0] // tiles
    y = y_ref[0]
    place = 0
    for piece in pieces:
        for b in range(piece.shape[0] // height):
            to = lax.rem(y + (STEPS[place] + tiles), tiles)
            q_ref[pl.ds(to * height, height), :] = piece[b * height : (b + 1) * height, :]
            place += 1
    place = lax.broadcasted_iota(jnp.int32, (sources, span), 1)
    which = lax.broadcasted_iota(jnp.int32, (sources, span), 0)
    spread = (place // PAGE == which).astype(jnp.bfloat16)
    fields = lax.dot_general(
        info_ref[...], spread, (((0,), (0,)), ((), ())), preferred_element_type=jnp.float32
    )
    within = lax.rem(lax.broadcasted_iota(jnp.int32, (1, span), 1), PAGE).astype(jnp.float32)
    q = q_ref[...]
    for o in range(kv_ref.shape[0] // sources):
        keys = kv_ref[o * sources : (o + 1) * sources, 0].reshape(span, hd)
        values = kv_ref[o * sources : (o + 1) * sources, 1].reshape(span, hd)
        seen = fields[o * FIELDS : o * FIELDS + tiles]
        live = fields[o * FIELDS + LIVE : o * FIELDS + LIVE + 1]
        allowed = jnp.where(within < live, seen, 0.0).astype(jnp.bfloat16)
        score = lax.dot_general(q, keys, (((1,), (1,)), ((), ())), preferred_element_type=jnp.float32)
        weight = silu(score * scale).astype(jnp.bfloat16)
        weight = weight.reshape(tiles, height, span) * allowed[:, None, :]
        part = jnp.dot(weight.reshape(tiles * height, span), values, preferred_element_type=jnp.float32)
        if o == 0:
            acc_ref[...] = part
        else:
            acc_ref[...] += part
    out_ref[...] = acc_ref[...].astype(out_ref.dtype)


def attend(y, info, pages, pieces, scale):
    rows, hd = sum(piece.shape[0] for piece in pieces), pages.shape[-1]
    return pl.pallas_call(
        functools.partial(attend_kernel, scale),
        in_specs=[SMEM] + [VMEM] * (2 + len(pieces)),
        out_specs=VMEM,
        out_shape=jax.ShapeDtypeStruct((rows, hd), jnp.bfloat16),
        scratch_shapes=[pltpu.VMEM((rows, hd), jnp.bfloat16), pltpu.VMEM((rows, hd), jnp.float32)],
        compiler_params=pltpu.CompilerParams(vmem_limit_bytes=40 * 1024 * 1024),
        name="attend",
    )(y, info, pages, *pieces)


def finish_kernel(scale, back_ref, proj_ref, input_ref, gain_ref, weight_ref, out_ref):
    rows, width = input_ref.shape
    hd = width // HEADS

    def act(block, h):
        start = block * width + h * hd
        value = silu(proj_ref[:, start : start + hd].astype(jnp.float32))
        return value.astype(jnp.bfloat16).astype(jnp.float32)

    attn = []
    for h in range(HEADS):
        total = jnp.zeros((rows, hd), jnp.float32)
        for g in range(back_ref.shape[0] // HEADS):
            total += back_ref[g * HEADS + h].astype(jnp.float32)
        own = silu(jnp.sum(act(2, h) * act(3, h), axis=1, keepdims=True) * scale)
        own = own.astype(jnp.bfloat16).astype(jnp.float32)
        attn.append(total + own * act(1, h))
    attn = jnp.concatenate(attn, axis=1)
    mean = jnp.mean(attn, axis=1, keepdims=True)
    centered = attn - mean
    var = jnp.mean(centered * centered, axis=1, keepdims=True)
    u_act = jnp.concatenate([act(0, h) for h in range(HEADS)], axis=1)
    normed = (centered * lax.rsqrt(var + eps) * gain_ref[...] * u_act).astype(jnp.bfloat16)
    out = jnp.dot(normed, weight_ref[...], preferred_element_type=jnp.float32)
    out_ref[...] = (input_ref[...].astype(jnp.float32) + out).astype(out_ref.dtype)


def finish(back, cand_proj, cand_input, out_gain, out_weight, scale):
    return pl.pallas_call(
        functools.partial(finish_kernel, scale),
        in_specs=[VMEM] * 5,
        out_specs=VMEM,
        out_shape=jax.ShapeDtypeStruct(cand_input.shape, cand_input.dtype),
        compiler_params=pltpu.CompilerParams(vmem_limit_bytes=40 * 1024 * 1024),
        name="finish",
    )(back, cand_proj, cand_input, out_gain.reshape(1, -1), out_weight)


def on_device(
    cand_proj, cand_input, kv_pool, page_owner, page_slot, lengths, block_mask, out_gain, out_weight
):
    rows, width = cand_input.shape
    hd = width // HEADS
    scale = hd ** (-0.5)
    n_z = lax.axis_size("z")
    z, y, h = lax.axis_index("z"), lax.axis_index("y"), lax.axis_index(("x", "c"))
    place = jnp.stack([z, lax.axis_index(PLANE)])
    owners, own_slots = page_owner.reshape(-1), page_slot.reshape(-1)

    sent = announce(place, owners, own_slots, lengths, block_mask[0], cand_proj, n_z)
    told = exchange(sent, SPREAD).reshape(n_z, HEADS, rows, hd)
    to_me = lax.dynamic_slice(told, (0, h, 0, z * FIELDS + SLOT), (n_z, 1, 1, 1)).reshape(-1)
    at_home = jnp.sum(jnp.where(owners == z, own_slots, 0))
    slots = jnp.where(jnp.arange(n_z) == z, at_home, to_me.astype(jnp.int32))
    pages = split_pages(jnp.clip(slots, 0, kv_pool.shape[0] - 1), kv_pool)
    pages, told = lax.optimization_barrier((pages, told))
    got = exchange(pages, SPREAD)
    below = lax.dynamic_slice(told, ((z + n_z - 1) % n_z, 0, 0, 0), (1, HEADS, 1, hd)).reshape(HEADS, hd)
    info = shift(below, "z", -1)
    pieces = gather_queries(lax.dynamic_index_in_dim(told, z, 0, keepdims=False).reshape(-1, hd))
    part = attend(y.reshape(1), info, got, pieces, scale)
    back = exchange(part.reshape(-1, rows, hd), PLANE)
    return finish(back, cand_proj, cand_input, out_gain, out_weight, scale)


def solution(mesh):
    n_z, n_p = mesh.shape["batch"], mesh.shape["pos"]
    cores, n_x = 2, HEADS // 2
    grid = Mesh(mesh.devices.reshape(n_z, n_p // HEADS, n_x, cores), ("z", "y", "x", "c"))
    rows = P(("z", "y", "x", "c"), None)
    placed = (
        rows,
        rows,
        P("z", None, PLANE, None),
        P("z", PLANE, None),
        P("z", PLANE, None),
        P("z"),
        P("z", None, PLANE),
        P(),
        P(),
    )
    return jax.shard_map(on_device, mesh=grid, in_specs=placed, out_specs=rows, check_vma=False)
```

```python
import functools

import jax
import jax.numpy as jnp
from jax import lax
from jax.experimental import pallas as pl
from jax.experimental.pallas import tpu as pltpu
from jax.sharding import Mesh
from jax.sharding import PartitionSpec as P

HEADS = 8
PAGE = 32
eps = 1e-05

PLANE = ("y", "x", "c")
SPREAD = ("z", "x", "c")
PAGES = ("x", "z", "c")
SUMS = ("x", "y", "c")
CORES = 2

FIELDS = 16
LIVE, SLOT = 8, 9

VMEM = pl.BlockSpec(memory_space=pltpu.VMEM)
SMEM = pl.BlockSpec(memory_space=pltpu.SMEM)
HBM = pl.BlockSpec(memory_space=pl.ANY)


def exchange(array, axes):
    return lax.all_to_all(array, axes, split_axis=0, concat_axis=0, tiled=True)


def shift(array, axis, step):
    n = lax.axis_size(axis)
    return lax.ppermute(array, axis, [(i, (i + step) % n) for i in range(n)])


def silu(value):
    half = value * 0.5
    return half + half * jnp.tanh(half)


def announce_kernel(owner_ref, slot_ref, length_ref, seen_ref, q_ref, out_ref):
    rows, hd = out_ref.shape[1:]
    pages = owner_ref.shape[0]
    blocks, tiles = seen_ref.shape
    place = lax.axis_index(PLANE)
    lane = lax.broadcasted_iota(jnp.int32, (rows, hd), 1)
    owner, field = lane // FIELDS, lane % FIELDS
    seen = []
    for b in range(blocks):
        row = jnp.zeros((rows, hd), jnp.int32)
        for t in range(tiles):
            row = jnp.where(field == t, seen_ref[b : b + 1, t : t + 1], row)
        seen.append(row)
    info = jnp.zeros((rows, hd), jnp.int32)
    for j in range(pages):
        live = jnp.clip(length_ref[0] - (place * pages + j) * PAGE, 0, PAGE)
        row = jnp.where(field == LIVE, live, seen[j * blocks // pages])
        row = jnp.where(field == SLOT, slot_ref[j], row)
        info = jnp.where(owner == owner_ref[j], row, info)
    info = info.astype(jnp.float32).astype(jnp.bfloat16)
    for i in range(out_ref.shape[0]):
        out_ref[i] = info
    query = silu(q_ref[...].astype(jnp.float32)).astype(jnp.bfloat16)
    for h in range(HEADS):
        out_ref[lax.axis_index("z") * HEADS + h] = query[:, h * hd : (h + 1) * hd]


def announce(owners, slots, lengths, seen, cand_proj, users):
    rows, width = cand_proj.shape[0], cand_proj.shape[1] // 4
    hd = width // HEADS
    return pl.pallas_call(
        announce_kernel,
        grid=(1,),
        in_specs=[SMEM] * 3 + [VMEM, pl.BlockSpec((rows, width), lambda i: (0, 2))],
        out_specs=VMEM,
        out_shape=jax.ShapeDtypeStruct((users * HEADS, rows, hd), jnp.bfloat16),
        name="announce",
    )(owners, slots, lengths, seen, cand_proj)


def split_pages_kernel(owner_ref, slot_ref, told_ref, pool_ref, out_ref, split_ref, sems):
    n_x, users = out_ref.shape[:2]
    rows, hd = told_ref.shape[1:]
    z, h = lax.axis_index("z"), lax.axis_index(("x", "c"))
    at_home = jnp.int32(0)
    for j in range(owner_ref.shape[0]):
        at_home = jnp.where(owner_ref[j] == z, slot_ref[j], at_home)
    lane = lax.broadcasted_iota(jnp.int32, (rows, hd), 1)
    row = lax.broadcasted_iota(jnp.int32, (rows, hd), 0)
    here = (row == 0) & (lane == z * FIELDS + SLOT)
    slots = []
    for u in range(users):
        told = told_ref[u * HEADS + h].astype(jnp.float32)
        slot = jnp.sum(jnp.where(here, told, 0.0)).astype(jnp.int32)
        slots.append(jnp.clip(jnp.where(z == u, at_home, slot), 0, pool_ref.shape[0] - 1))
    copies = []
    for u in range(users):
        for k in range(HEADS):
            split_ref[k // CORES, u, k % CORES] = pool_ref[slots[u], :, :, k * hd : (k + 1) * hd]
        copies.append(pltpu.make_async_copy(split_ref.at[:, u], out_ref.at[:, u], sems.at[u]))
        copies[-1].start()
    for copy in copies:
        copy.wait()


def split_pages(owners, own_slots, told, kv_pool):
    _, _, page, width = kv_pool.shape
    users = told.shape[0] // HEADS
    shape = (HEADS // CORES, users, CORES, 2, page, width // HEADS)
    return pl.pallas_call(
        split_pages_kernel,
        in_specs=[SMEM, SMEM, VMEM, VMEM],
        out_specs=HBM,
        out_shape=jax.ShapeDtypeStruct(shape, kv_pool.dtype),
        scratch_shapes=[pltpu.VMEM(shape, kv_pool.dtype), pltpu.SemaphoreType.DMA((users,))],
        name="split_pages",
    )(owners, own_slots, told, kv_pool)


STEPS = (0, -1, 1, -3, -4, -2, 3, 2)


def gather_queries(row):
    below, above = shift(row, "y", 1), shift(row, "y", -1)
    below3 = shift(jnp.concatenate([row, below, above]), "y", 3)
    above3 = shift(jnp.concatenate([row, below]), "y", -3)
    return row, below, above, below3, above3


def attend_kernel(scale, info_ref, kv_ref, *rest):
    pieces, (out_ref, q_ref, acc_ref) = rest[:-3], rest[-3:]
    n_x, n_y, cores, rows, hd = out_ref.shape
    sources, tiles = info_ref.shape[0], len(STEPS)
    span = sources * PAGE
    height = n_x * cores * rows
    y = lax.axis_index("y")
    place = 0
    for piece in pieces:
        for b in range(piece.shape[0] // height):
            to = lax.rem(y + (STEPS[place] + tiles), tiles)
            q_ref[pl.ds(to * height, height), :] = piece[b * height : (b + 1) * height, :]
            place += 1
    place = lax.broadcasted_iota(jnp.int32, (sources, span), 1)
    which = lax.broadcasted_iota(jnp.int32, (sources, span), 0)
    spread = (place // PAGE == which).astype(jnp.bfloat16)
    fields = lax.dot_general(
        info_ref[...], spread, (((0,), (0,)), ((), ())), preferred_element_type=jnp.float32
    )
    within = lax.rem(lax.broadcasted_iota(jnp.int32, (1, span), 1), PAGE).astype(jnp.float32)
    q = q_ref[...]
    for o in range(kv_ref.shape[1]):
        keys = kv_ref[:, o, :, 0].reshape(span, hd)
        values = kv_ref[:, o, :, 1].reshape(span, hd)
        seen = fields[o * FIELDS : o * FIELDS + tiles]
        live = fields[o * FIELDS + LIVE : o * FIELDS + LIVE + 1]
        allowed = jnp.where(within < live, seen, 0.0).astype(jnp.bfloat16)
        score = lax.dot_general(q, keys, (((1,), (1,)), ((), ())), preferred_element_type=jnp.float32)
        weight = silu(score * scale).astype(jnp.bfloat16)
        weight = weight.reshape(tiles, height, span) * allowed[:, None, :]
        part = jnp.dot(weight.reshape(tiles * height, span), values, preferred_element_type=jnp.float32)
        if o == 0:
            acc_ref[...] = part
        else:
            acc_ref[...] += part
    total = acc_ref[...].astype(out_ref.dtype).reshape(n_y, n_x, cores, rows, hd)
    for t in range(n_y):
        out_ref[:, t] = total[t]


def attend(info, pages, pieces, scale, rows):
    n_x, _, cores, _, _, hd = pages.shape
    height = sum(piece.shape[0] for piece in pieces)
    return pl.pallas_call(
        functools.partial(attend_kernel, scale),
        in_specs=[VMEM] * (2 + len(pieces)),
        out_specs=VMEM,
        out_shape=jax.ShapeDtypeStruct((n_x, len(STEPS), cores, rows, hd), jnp.bfloat16),
        scratch_shapes=[pltpu.VMEM((height, hd), jnp.bfloat16), pltpu.VMEM((height, hd), jnp.float32)],
        compiler_params=pltpu.CompilerParams(vmem_limit_bytes=40 * 1024 * 1024),
        name="attend",
    )(info, pages, *pieces)


def finish_kernel(scale, back_ref, proj_ref, input_ref, gain_ref, weight_ref, out_ref):
    rows, width = input_ref.shape
    hd = width // HEADS

    def act(block, h):
        start = block * width + h * hd
        value = silu(proj_ref[:, start : start + hd].astype(jnp.float32))
        return value.astype(jnp.bfloat16).astype(jnp.float32)

    attn = []
    for h in range(HEADS):
        total = jnp.zeros((rows, hd), jnp.float32)
        for y in range(back_ref.shape[1]):
            total += back_ref[h // CORES, y, h % CORES].astype(jnp.float32)
        own = silu(jnp.sum(act(2, h) * act(3, h), axis=1, keepdims=True) * scale)
        own = own.astype(jnp.bfloat16).astype(jnp.float32)
        attn.append(total + own * act(1, h))
    attn = jnp.concatenate(attn, axis=1)
    mean = jnp.mean(attn, axis=1, keepdims=True)
    centered = attn - mean
    var = jnp.mean(centered * centered, axis=1, keepdims=True)
    u_act = jnp.concatenate([act(0, h) for h in range(HEADS)], axis=1)
    normed = (centered * lax.rsqrt(var + eps) * gain_ref[...] * u_act).astype(jnp.bfloat16)
    out = jnp.dot(normed, weight_ref[...], preferred_element_type=jnp.float32)
    out_ref[...] = (input_ref[...].astype(jnp.float32) + out).astype(out_ref.dtype)


def finish(back, cand_proj, cand_input, out_gain, out_weight, scale):
    return pl.pallas_call(
        functools.partial(finish_kernel, scale),
        in_specs=[VMEM] * 5,
        out_specs=VMEM,
        out_shape=jax.ShapeDtypeStruct(cand_input.shape, cand_input.dtype),
        compiler_params=pltpu.CompilerParams(vmem_limit_bytes=40 * 1024 * 1024),
        name="finish",
    )(back, cand_proj, cand_input, out_gain.reshape(1, -1), out_weight)


def on_device(
    cand_proj, cand_input, kv_pool, page_owner, page_slot, lengths, block_mask, out_gain, out_weight
):
    rows, width = cand_input.shape
    hd = width // HEADS
    scale = hd ** (-0.5)
    n_z = lax.axis_size("z")
    z = lax.axis_index("z")
    owners, own_slots = page_owner.reshape(-1), page_slot.reshape(-1)

    sent = announce(owners, own_slots, lengths, block_mask[0].T, cand_proj, n_z)
    told = exchange(sent, SPREAD)
    pages = split_pages(owners, own_slots, told, kv_pool)
    pages, told = lax.optimization_barrier((pages, told))
    got = exchange(pages.reshape((-1,) + pages.shape[3:]), PAGES).reshape(pages.shape)
    told = told.reshape(n_z, HEADS, rows, hd)
    below = lax.dynamic_slice(told, ((z + n_z - 1) % n_z, 0, 0, 0), (1, HEADS, 1, hd)).reshape(HEADS, hd)
    info = shift(below, "z", -1)
    pieces = gather_queries(lax.dynamic_index_in_dim(told, z, 0, keepdims=False).reshape(-1, hd))
    part = attend(info, got, pieces, scale, rows)
    back = exchange(part.reshape(-1, rows, hd), SUMS).reshape(part.shape)
    return finish(back, cand_proj, cand_input, out_gain, out_weight, scale)


def solution(mesh):
    n_z, n_p = mesh.shape["batch"], mesh.shape["pos"]
    n_x = HEADS // CORES
    grid = Mesh(mesh.devices.reshape(n_z, n_p // HEADS, n_x, CORES), ("z", "y", "x", "c"))
    rows = P(("z", "y", "x", "c"), None)
    placed = (
        rows,
        rows,
        P("z", None, PLANE, None),
        P("z", PLANE, None),
        P("z", PLANE, None),
        P("z"),
        P("z", None, PLANE),
        P(),
        P(),
    )
    return jax.shard_map(on_device, mesh=grid, in_specs=placed, out_specs=rows, check_vma=False)
```

```python
import functools

import jax
import jax.numpy as jnp
from jax import lax
from jax.experimental import pallas as pl
from jax.experimental.pallas import tpu as pltpu
from jax.sharding import Mesh
from jax.sharding import PartitionSpec as P

HEADS = 8
PAGE = 32
eps = 1e-05

PLANE = ("y", "x", "c")
SPREAD = ("z", "x", "c")
PAGES = ("x", "z", "c")
SUMS = ("x", "y", "c")
CORES = 2

FIELDS = 16
LIVE, SLOT = 8, 9

VMEM = pl.BlockSpec(memory_space=pltpu.VMEM)
SMEM = pl.BlockSpec(memory_space=pltpu.SMEM)
HBM = pl.BlockSpec(memory_space=pl.ANY)


def exchange(array, axes):
    return lax.all_to_all(array, axes, split_axis=0, concat_axis=0, tiled=True)


def shift(array, axis, step):
    n = lax.axis_size(axis)
    return lax.ppermute(array, axis, [(i, (i + step) % n) for i in range(n)])


def silu(value):
    half = value * 0.5
    return half + half * jnp.tanh(half)


def announce_kernel(owner_ref, slot_ref, length_ref, seen_ref, out_ref):
    rows, hd = out_ref.shape[1:]
    pages = owner_ref.shape[0]
    blocks, tiles = seen_ref.shape
    place = lax.axis_index(PLANE)
    lane = lax.broadcasted_iota(jnp.int32, (rows, hd), 1)
    owner, field = lane // FIELDS, lane % FIELDS
    seen = []
    for b in range(blocks):
        row = jnp.zeros((rows, hd), jnp.int32)
        for t in range(tiles):
            row = jnp.where(field == t, seen_ref[b : b + 1, t : t + 1], row)
        seen.append(row)
    info = jnp.zeros((rows, hd), jnp.int32)
    for j in range(pages):
        live = jnp.clip(length_ref[0] - (place * pages + j) * PAGE, 0, PAGE)
        row = jnp.where(field == LIVE, live, seen[j * blocks // pages])
        row = jnp.where(field == SLOT, slot_ref[j], row)
        info = jnp.where(owner == owner_ref[j], row, info)
    info = info.astype(jnp.float32).astype(jnp.bfloat16)
    for i in range(out_ref.shape[0]):
        out_ref[i] = info


def announce(owners, slots, lengths, seen, users, rows, hd):
    return pl.pallas_call(
        announce_kernel,
        in_specs=[SMEM] * 3 + [VMEM],
        out_specs=VMEM,
        out_shape=jax.ShapeDtypeStruct((users, rows, hd), jnp.bfloat16),
        name="announce",
    )(owners, slots, lengths, seen)


def ask_kernel(q_ref, info_ref, out_ref):
    rows, hd = info_ref.shape[1:]
    query = silu(q_ref[...].astype(jnp.float32)).astype(jnp.bfloat16)
    for h in range(HEADS):
        out_ref[h, :rows] = query[:, h * hd : (h + 1) * hd]
        out_ref[h, rows:] = info_ref[0]


def ask(cand_proj, info):
    rows, width = cand_proj.shape[0], cand_proj.shape[1] // 4
    hd = width // HEADS
    return pl.pallas_call(
        ask_kernel,
        grid=(1,),
        in_specs=[pl.BlockSpec((rows, width), lambda i: (0, 2)), VMEM],
        out_specs=VMEM,
        out_shape=jax.ShapeDtypeStruct((HEADS, 2 * rows, hd), jnp.bfloat16),
        name="ask",
    )(cand_proj, info)


def split_pages_kernel(told_ref, pool_ref, out_ref, split_ref, sems):
    n_x, users = out_ref.shape[:2]
    rows, hd = told_ref.shape[1:]
    lane = lax.broadcasted_iota(jnp.int32, (rows, hd), 1)
    row = lax.broadcasted_iota(jnp.int32, (rows, hd), 0)
    here = (row == 0) & (lane == lax.axis_index("z") * FIELDS + SLOT)
    slots = []
    for u in range(users):
        slot = jnp.sum(jnp.where(here, told_ref[u].astype(jnp.float32), 0.0)).astype(jnp.int32)
        slots.append(jnp.clip(slot, 0, pool_ref.shape[0] - 1))
    copies = []
    for u in range(users):
        for k in range(HEADS):
            split_ref[k // CORES, u, k % CORES] = pool_ref[slots[u], :, :, k * hd : (k + 1) * hd]
        copies.append(pltpu.make_async_copy(split_ref.at[:, u], out_ref.at[:, u], sems.at[u]))
        copies[-1].start()
    for copy in copies:
        copy.wait()


def split_pages(told, kv_pool):
    _, _, page, width = kv_pool.shape
    shape = (HEADS // CORES, told.shape[0], CORES, 2, page, width // HEADS)
    return pl.pallas_call(
        split_pages_kernel,
        in_specs=[VMEM, VMEM],
        out_specs=HBM,
        out_shape=jax.ShapeDtypeStruct(shape, kv_pool.dtype),
        scratch_shapes=[pltpu.VMEM(shape, kv_pool.dtype), pltpu.SemaphoreType.DMA((told.shape[0],))],
        name="split_pages",
    )(told, kv_pool)


STEPS = (0, -3, 3, -1, -4, 2, 1, -2)


def gather_queries(row):
    below3, above3 = shift(row, "y", 3), shift(row, "y", -3)
    below = shift(jnp.concatenate([row, below3, above3]), "y", 1)
    above = shift(jnp.concatenate([row, below3]), "y", -1)
    return below3, above3, below, above


def attend_kernel(scale, asked_ref, kv_ref, *rest):
    pieces, (out_ref, q_ref, acc_ref) = rest[:-3], rest[-3:]
    n_x, n_y, cores, rows, hd = out_ref.shape
    sources, tiles = n_x * cores, len(STEPS)
    span = sources * PAGE
    height = n_x * cores * rows
    y = lax.axis_index("y")
    blocks = [asked_ref[:, :rows].reshape(height, hd)]
    for piece in pieces:
        blocks += [piece[b * height : (b + 1) * height, :] for b in range(piece.shape[0] // height)]
    for step, block in zip(STEPS, blocks):
        q_ref[pl.ds(lax.rem(y + (step + tiles), tiles) * height, height), :] = block
    place = lax.broadcasted_iota(jnp.int32, (height, span), 1)
    which = lax.broadcasted_iota(jnp.int32, (height, span), 0)
    spread = (place // PAGE * rows == which).astype(jnp.bfloat16)
    fields = lax.dot_general(
        asked_ref[:, rows:].reshape(height, hd), spread, (((0,), (0,)), ((), ())), preferred_element_type=jnp.float32
    )
    within = lax.rem(lax.broadcasted_iota(jnp.int32, (1, span), 1), PAGE).astype(jnp.float32)
    q = q_ref[...]
    for o in range(kv_ref.shape[1]):
        keys = kv_ref[:, o, :, 0].reshape(span, hd)
        values = kv_ref[:, o, :, 1].reshape(span, hd)
        seen = fields[o * FIELDS : o * FIELDS + tiles]
        live = fields[o * FIELDS + LIVE : o * FIELDS + LIVE + 1]
        allowed = jnp.where(within < live, seen, 0.0).astype(jnp.bfloat16)
        score = lax.dot_general(q, keys, (((1,), (1,)), ((), ())), preferred_element_type=jnp.float32)
        weight = silu(score * scale).astype(jnp.bfloat16)
        weight = weight.reshape(tiles, height, span) * allowed[:, None, :]
        part = jnp.dot(weight.reshape(tiles * height, span), values, preferred_element_type=jnp.float32)
        if o == 0:
            acc_ref[...] = part
        else:
            acc_ref[...] += part
    total = acc_ref[...].astype(out_ref.dtype).reshape(n_y, n_x, cores, rows, hd)
    for t in range(n_y):
        out_ref[:, t] = total[t]


def attend(asked, pages, pieces, scale):
    n_x, _, cores, _, _, hd = pages.shape
    rows = asked.shape[1] // 2
    out = jax.ShapeDtypeStruct((n_x, len(STEPS), cores, rows, hd), jnp.bfloat16)
    height = out.size // hd
    return pl.pallas_call(
        functools.partial(attend_kernel, scale),
        in_specs=[VMEM] * (2 + len(pieces)),
        out_specs=VMEM,
        out_shape=out,
        scratch_shapes=[pltpu.VMEM((height, hd), jnp.bfloat16), pltpu.VMEM((height, hd), jnp.float32)],
        compiler_params=pltpu.CompilerParams(vmem_limit_bytes=16 * 1024 * 1024),
        name="attend",
    )(asked, pages, *pieces)


def finish_kernel(scale, back_ref, proj_ref, input_ref, gain_ref, weight_ref, out_ref):
    rows, width = input_ref.shape
    hd = width // HEADS

    def act(block, h):
        start = block * width + h * hd
        value = silu(proj_ref[:, start : start + hd].astype(jnp.float32))
        return value.astype(jnp.bfloat16).astype(jnp.float32)

    attn = []
    for h in range(HEADS):
        total = jnp.zeros((rows, hd), jnp.float32)
        for y in range(back_ref.shape[1]):
            total += back_ref[h // CORES, y, h % CORES].astype(jnp.float32)
        own = silu(jnp.sum(act(2, h) * act(3, h), axis=1, keepdims=True) * scale)
        own = own.astype(jnp.bfloat16).astype(jnp.float32)
        attn.append(total + own * act(1, h))
    attn = jnp.concatenate(attn, axis=1)
    mean = jnp.mean(attn, axis=1, keepdims=True)
    centered = attn - mean
    var = jnp.mean(centered * centered, axis=1, keepdims=True)
    u_act = jnp.concatenate([act(0, h) for h in range(HEADS)], axis=1)
    normed = (centered * lax.rsqrt(var + eps) * gain_ref[...] * u_act).astype(jnp.bfloat16)
    out = jnp.dot(normed, weight_ref[...], preferred_element_type=jnp.float32)
    out_ref[...] = (input_ref[...].astype(jnp.float32) + out).astype(out_ref.dtype)


def finish(back, cand_proj, cand_input, out_gain, out_weight, scale):
    return pl.pallas_call(
        functools.partial(finish_kernel, scale),
        in_specs=[VMEM] * 5,
        out_specs=VMEM,
        out_shape=jax.ShapeDtypeStruct(cand_input.shape, cand_input.dtype),
        compiler_params=pltpu.CompilerParams(vmem_limit_bytes=16 * 1024 * 1024),
        name="finish",
    )(back, cand_proj, cand_input, out_gain.reshape(1, -1), out_weight)


def on_device(
    cand_proj, cand_input, kv_pool, page_owner, page_slot, lengths, block_mask, out_gain, out_weight
):
    rows, width = cand_input.shape
    hd = width // HEADS
    scale = hd ** (-0.5)
    n_z = lax.axis_size("z")
    owners, own_slots = page_owner.reshape(-1), page_slot.reshape(-1)

    sent = announce(owners, own_slots, lengths, block_mask[0].T, n_z, rows, hd)
    told = exchange(sent, ("z",))
    told, asked = lax.optimization_barrier((told, ask(cand_proj, sent)))
    asked = exchange(asked, ("x", "c"))
    pages = split_pages(told, kv_pool)
    pages, asked = lax.optimization_barrier((pages, asked))
    got = exchange(pages.reshape((-1,) + pages.shape[3:]), PAGES).reshape(pages.shape)
    pieces = gather_queries(asked[:, :rows].reshape(-1, hd))
    part = attend(asked, got, pieces, scale)
    back = exchange(part.reshape(-1, rows, hd), SUMS).reshape(part.shape)
    return finish(back, cand_proj, cand_input, out_gain, out_weight, scale)


def solution(mesh):
    n_z, n_p = mesh.shape["batch"], mesh.shape["pos"]
    n_x = HEADS // CORES
    grid = Mesh(mesh.devices.reshape(n_z, n_p // HEADS, n_x, CORES), ("z", "y", "x", "c"))
    rows = P(("z", "y", "x", "c"), None)
    placed = (
        rows,
        rows,
        P("z", None, PLANE, None),
        P("z", PLANE, None),
        P("z", PLANE, None),
        P("z"),
        P("z", None, PLANE),
        P(),
        P(),
    )
    return jax.shard_map(on_device, mesh=grid, in_specs=placed, out_specs=rows, check_vma=False)
```

```python
import functools

import jax
import jax.numpy as jnp
from jax import lax
from jax.experimental import pallas as pl
from jax.experimental.pallas import tpu as pltpu
from jax.sharding import Mesh
from jax.sharding import PartitionSpec as P

HEADS = 8
PAGE = 32
eps = 1e-05

PLANE = ("y", "x", "c")
SPREAD = ("z", "x", "c")
PAGES = ("x", "z", "c")
SUMS = ("x", "y", "c")
CORES = 2

FIELDS = 16
LIVE, SLOT = 8, 9

VMEM = pl.BlockSpec(memory_space=pltpu.VMEM)
SMEM = pl.BlockSpec(memory_space=pltpu.SMEM)
HBM = pl.BlockSpec(memory_space=pl.ANY)


def exchange(array, axes):
    return lax.all_to_all(array, axes, split_axis=0, concat_axis=0, tiled=True)


def shift(array, axis, step):
    n = lax.axis_size(axis)
    return lax.ppermute(array, axis, [(i, (i + step) % n) for i in range(n)])


def silu(value):
    half = value * 0.5
    return half + half * jnp.tanh(half)


def announce_kernel(owner_ref, slot_ref, length_ref, seen_ref, out_ref):
    rows, hd = out_ref.shape[1:]
    pages = owner_ref.shape[0]
    blocks, tiles = seen_ref.shape
    place = lax.axis_index(PLANE)
    lane = lax.broadcasted_iota(jnp.int32, (rows, hd), 1)
    owner, field = lane // FIELDS, lane % FIELDS
    seen = []
    for b in range(blocks):
        row = jnp.zeros((rows, hd), jnp.int32)
        for t in range(tiles):
            row = jnp.where(field == t, seen_ref[b : b + 1, t : t + 1], row)
        seen.append(row)
    info = jnp.zeros((rows, hd), jnp.int32)
    for j in range(pages):
        live = jnp.clip(length_ref[0] - (place * pages + j) * PAGE, 0, PAGE)
        row = jnp.where(field == LIVE, live, seen[j * blocks // pages])
        row = jnp.where(field == SLOT, slot_ref[j], row)
        info = jnp.where(owner == owner_ref[j], row, info)
    info = info.astype(jnp.float32).astype(jnp.bfloat16)
    for i in range(out_ref.shape[0]):
        out_ref[i] = info


def announce(owners, slots, lengths, seen, users, rows, hd):
    return pl.pallas_call(
        announce_kernel,
        in_specs=[SMEM] * 3 + [VMEM],
        out_specs=VMEM,
        out_shape=jax.ShapeDtypeStruct((users, rows, hd), jnp.bfloat16),
        name="announce",
    )(owners, slots, lengths, seen)


def ask_kernel(scale, proj_ref, info_ref, out_ref, own_ref, u_ref):
    rows, hd = info_ref.shape[1:]

    def act(block, h):
        start = (block * HEADS + h) * hd
        return silu(proj_ref[:, start : start + hd].astype(jnp.float32)).astype(jnp.bfloat16)

    for h in range(HEADS):
        part = slice(h * hd, (h + 1) * hd)
        query = act(2, h)
        out_ref[h, :rows] = query
        out_ref[h, rows:] = info_ref[0]
        score = query.astype(jnp.float32) * act(3, h).astype(jnp.float32)
        own = silu(jnp.sum(score, axis=1, keepdims=True) * scale).astype(jnp.bfloat16)
        own_ref[:, part] = own.astype(jnp.float32) * act(1, h).astype(jnp.float32)
        u_ref[:, part] = act(0, h)


def ask(cand_proj, info, scale):
    rows, hd = info.shape[1:]
    width = cand_proj.shape[1] // 4
    return pl.pallas_call(
        functools.partial(ask_kernel, scale),
        in_specs=[VMEM] * 2,
        out_specs=[VMEM] * 3,
        out_shape=[
            jax.ShapeDtypeStruct((HEADS, 2 * rows, hd), jnp.bfloat16),
            jax.ShapeDtypeStruct((rows, width), jnp.float32),
            jax.ShapeDtypeStruct((rows, width), jnp.bfloat16),
        ],
        name="ask",
    )(cand_proj, info)


def split_pages_kernel(told_ref, pool_ref, out_ref, split_ref, sems):
    n_x, users = out_ref.shape[:2]
    rows, hd = told_ref.shape[1:]
    lane = lax.broadcasted_iota(jnp.int32, (rows, hd), 1)
    row = lax.broadcasted_iota(jnp.int32, (rows, hd), 0)
    here = (row == 0) & (lane == lax.axis_index("z") * FIELDS + SLOT)
    slots = []
    for u in range(users):
        slot = jnp.sum(jnp.where(here, told_ref[u].astype(jnp.float32), 0.0)).astype(jnp.int32)
        slots.append(jnp.clip(slot, 0, pool_ref.shape[0] - 1))
    copies = []
    for u in range(users):
        for k in range(HEADS):
            split_ref[k // CORES, u, k % CORES] = pool_ref[slots[u], :, :, k * hd : (k + 1) * hd]
        copies.append(pltpu.make_async_copy(split_ref.at[:, u], out_ref.at[:, u], sems.at[u]))
        copies[-1].start()
    for copy in copies:
        copy.wait()


def split_pages(told, kv_pool):
    _, _, page, width = kv_pool.shape
    shape = (HEADS // CORES, told.shape[0], CORES, 2, page, width // HEADS)
    return pl.pallas_call(
        split_pages_kernel,
        in_specs=[VMEM, VMEM],
        out_specs=HBM,
        out_shape=jax.ShapeDtypeStruct(shape, kv_pool.dtype),
        scratch_shapes=[pltpu.VMEM(shape, kv_pool.dtype), pltpu.SemaphoreType.DMA((told.shape[0],))],
        name="split_pages",
    )(told, kv_pool)


STEPS = (0, -1, 1, -3, -2, 3, 4, 2)


def gather_queries(row):
    below, above = shift(row, "y", 1), shift(row, "y", -1)
    below3 = shift(jnp.concatenate([row, above]), "y", 3)
    above3 = shift(jnp.concatenate([row, above, below]), "y", -3)
    return below, above, below3, above3


def attend_kernel(scale, info_ref, row_ref, kv_ref, *rest):
    pieces, (out_ref, q_ref, acc_ref) = rest[:-3], rest[-3:]
    n_x, n_y, cores, rows, hd = out_ref.shape
    sources, tiles = n_x * cores, len(STEPS)
    span = sources * PAGE
    height = n_x * cores * rows
    y = lax.axis_index("y")
    blocks = [row_ref[...]]
    for piece in pieces:
        blocks += [piece[b * height : (b + 1) * height, :] for b in range(piece.shape[0] // height)]
    for step, block in zip(STEPS, blocks):
        q_ref[pl.ds(lax.rem(y + (step + tiles), tiles) * height, height), :] = block
    place = lax.broadcasted_iota(jnp.int32, (sources, span), 1)
    which = lax.broadcasted_iota(jnp.int32, (sources, span), 0)
    spread = (place // PAGE == which).astype(jnp.bfloat16)
    fields = lax.dot_general(
        info_ref[...], spread, (((0,), (0,)), ((), ())), preferred_element_type=jnp.float32
    )
    within = lax.rem(lax.broadcasted_iota(jnp.int32, (1, span), 1), PAGE).astype(jnp.float32)
    q = q_ref[...]
    for o in range(kv_ref.shape[1]):
        keys = kv_ref[:, o, :, 0].reshape(span, hd)
        values = kv_ref[:, o, :, 1].reshape(span, hd)
        seen = fields[o * FIELDS : o * FIELDS + tiles]
        live = fields[o * FIELDS + LIVE : o * FIELDS + LIVE + 1]
        allowed = jnp.where(within < live, seen, 0.0).astype(jnp.bfloat16)
        score = lax.dot_general(q, keys, (((1,), (1,)), ((), ())), preferred_element_type=jnp.float32)
        weight = silu(score * scale).astype(jnp.bfloat16)
        weight = weight.reshape(tiles, height, span) * allowed[:, None, :]
        part = jnp.dot(weight.reshape(tiles * height, span), values, preferred_element_type=jnp.float32)
        if o == 0:
            acc_ref[...] = part
        else:
            acc_ref[...] += part
    total = acc_ref[...].astype(out_ref.dtype).reshape(n_y, n_x, cores, rows, hd)
    for t in range(n_y):
        out_ref[:, t] = total[t]


def attend(info, row, pages, pieces, scale):
    n_x, _, cores, _, _, hd = pages.shape
    rows = row.shape[0] // (n_x * cores)
    out = jax.ShapeDtypeStruct((n_x, len(STEPS), cores, rows, hd), jnp.bfloat16)
    height = out.size // hd
    return pl.pallas_call(
        functools.partial(attend_kernel, scale),
        in_specs=[VMEM] * (3 + len(pieces)),
        out_specs=VMEM,
        out_shape=out,
        scratch_shapes=[pltpu.VMEM((height, hd), jnp.bfloat16), pltpu.VMEM((height, hd), jnp.float32)],
        compiler_params=pltpu.CompilerParams(vmem_limit_bytes=16 * 1024 * 1024),
        name="attend",
    )(info, row, pages, *pieces)


def finish_kernel(back_ref, own_ref, u_ref, gain_ref, input_ref, weight_ref, out_ref):
    attn = []
    for h in range(HEADS):
        total = back_ref[h // CORES, 0, h % CORES].astype(jnp.float32)
        for y in range(1, back_ref.shape[1]):
            total += back_ref[h // CORES, y, h % CORES].astype(jnp.float32)
        attn.append(total)
    attn = jnp.concatenate(attn, axis=1) + own_ref[...]
    mean = jnp.mean(attn, axis=1, keepdims=True)
    centered = attn - mean
    var = jnp.mean(centered * centered, axis=1, keepdims=True)
    gate = gain_ref[...] * u_ref[...].astype(jnp.float32)
    normed = (centered * lax.rsqrt(var + eps) * gate).astype(jnp.bfloat16)
    out = jnp.dot(normed, weight_ref[...], preferred_element_type=jnp.float32)
    out_ref[...] = (input_ref[...].astype(jnp.float32) + out).astype(out_ref.dtype)


def finish(back, own, u_act, out_gain, cand_input, out_weight):
    return pl.pallas_call(
        finish_kernel,
        in_specs=[VMEM] * 6,
        out_specs=VMEM,
        out_shape=jax.ShapeDtypeStruct(cand_input.shape, cand_input.dtype),
        compiler_params=pltpu.CompilerParams(vmem_limit_bytes=16 * 1024 * 1024),
        name="finish",
    )(back, own, u_act, out_gain.reshape(1, -1), cand_input, out_weight)


def on_device(
    cand_proj, cand_input, kv_pool, page_owner, page_slot, lengths, block_mask, out_gain, out_weight
):
    rows, width = cand_input.shape
    hd = width // HEADS
    scale = hd ** (-0.5)
    n_z = lax.axis_size("z")
    owners, own_slots = page_owner.reshape(-1), page_slot.reshape(-1)

    sent = announce(owners, own_slots, lengths, block_mask[0].T, n_z, rows, hd)
    told = exchange(sent, ("z",))
    asked, own, u_act = ask(cand_proj, sent, scale)
    told, asked = lax.optimization_barrier((told, asked))
    asked = exchange(asked, ("x", "c"))
    pages = split_pages(told, kv_pool)
    pages, asked = lax.optimization_barrier((pages, asked))
    got = exchange(pages.reshape((-1,) + pages.shape[3:]), PAGES).reshape(pages.shape)
    row, info = asked[:, :rows].reshape(-1, hd), asked[:, rows]
    part = attend(info, row, got, gather_queries(row), scale)
    back = exchange(part.reshape(-1, rows, hd), SUMS).reshape(part.shape)
    return finish(back, own, u_act, out_gain, cand_input, out_weight)


def solution(mesh):
    n_z, n_p = mesh.shape["batch"], mesh.shape["pos"]
    n_x = HEADS // CORES
    grid = Mesh(mesh.devices.reshape(n_z, n_p // HEADS, n_x, CORES), ("z", "y", "x", "c"))
    rows = P(("z", "y", "x", "c"), None)
    placed = (
        rows,
        rows,
        P("z", None, PLANE, None),
        P("z", PLANE, None),
        P("z", PLANE, None),
        P("z"),
        P("z", None, PLANE),
        P(),
        P(),
    )
    return jax.shard_map(on_device, mesh=grid, in_specs=placed, out_specs=rows, check_vma=False)
```

```python
import functools

import jax
import jax.numpy as jnp
from jax import lax
from jax.experimental import pallas as pl
from jax.experimental.pallas import tpu as pltpu
from jax.sharding import Mesh
from jax.sharding import PartitionSpec as P

HEADS = 8
PAGE = 32
eps = 1e-05

PLANE = ("y", "x", "c")
SPREAD = ("z", "x", "c")
PAGES = ("x", "z", "c")
SUMS = ("x", "y", "c")
CORES = 2

FIELDS = 16
LIVE = 8

VMEM = pl.BlockSpec(memory_space=pltpu.VMEM)
SMEM = pl.BlockSpec(memory_space=pltpu.SMEM)
HBM = pl.BlockSpec(memory_space=pl.ANY)


def exchange(array, axes):
    return lax.all_to_all(array, axes, split_axis=0, concat_axis=0, tiled=True)


def shift(array, axis, step):
    n = lax.axis_size(axis)
    return lax.ppermute(array, axis, [(i, (i + step) % n) for i in range(n)])


def silu(value):
    half = value * 0.5
    return half + half * jnp.tanh(half)


def ask_kernel(scale, owner_ref, length_ref, seen_ref, proj_ref, out_ref, own_ref, u_ref):
    pages = owner_ref.shape[0]
    blocks, tiles = seen_ref.shape
    rows, hd = out_ref.shape[1] // 2, out_ref.shape[2]
    place = lax.axis_index(PLANE)
    lane = lax.broadcasted_iota(jnp.int32, (rows, hd), 1)
    owner, field = lane // FIELDS, lane % FIELDS
    seen = []
    for b in range(blocks):
        row = jnp.zeros((rows, hd), jnp.int32)
        for t in range(tiles):
            row = jnp.where(field == t, seen_ref[b : b + 1, t : t + 1], row)
        seen.append(row)
    info = jnp.zeros((rows, hd), jnp.int32)
    for j in range(pages):
        live = jnp.clip(length_ref[0] - (place * pages + j) * PAGE, 0, PAGE)
        row = jnp.where(field == LIVE, live, seen[j * blocks // pages])
        info = jnp.where(owner == owner_ref[j], row, info)
    info = info.astype(jnp.float32).astype(jnp.bfloat16)

    def act(block, h):
        start = (block * HEADS + h) * hd
        return silu(proj_ref[:, start : start + hd].astype(jnp.float32)).astype(jnp.bfloat16)

    for h in range(HEADS):
        part = slice(h * hd, (h + 1) * hd)
        query = act(2, h)
        out_ref[h, :rows] = query
        out_ref[h, rows:] = info
        score = query.astype(jnp.float32) * act(3, h).astype(jnp.float32)
        own = silu(jnp.sum(score, axis=1, keepdims=True) * scale).astype(jnp.bfloat16)
        own_ref[:, part] = own.astype(jnp.float32) * act(1, h).astype(jnp.float32)
        u_ref[:, part] = act(0, h)


def ask(owners, lengths, seen, cand_proj, scale):
    rows, width = cand_proj.shape[0], cand_proj.shape[1] // 4
    hd = width // HEADS
    return pl.pallas_call(
        functools.partial(ask_kernel, scale),
        in_specs=[SMEM] * 2 + [VMEM] * 2,
        out_specs=[VMEM] * 3,
        out_shape=[
            jax.ShapeDtypeStruct((HEADS, 2 * rows, hd), jnp.bfloat16),
            jax.ShapeDtypeStruct((rows, width), jnp.float32),
            jax.ShapeDtypeStruct((rows, width), jnp.bfloat16),
        ],
        name="ask",
    )(owners, lengths, seen, cand_proj)


def split_pages_kernel(told_ref, pool_ref, out_ref, split_ref, sems):
    n_x, users = out_ref.shape[:2]
    hd = out_ref.shape[5]
    count = pool_ref.shape[0]
    first = lax.axis_index("z") * count
    slots = []
    for u in range(users):
        slot = jnp.int32(0)
        for j in range(told_ref.shape[1]):
            at = told_ref[u, j] - first
            slot = jnp.where((at >= 0) & (at < count), at, slot)
        slots.append(slot)
    copies = []
    for u in range(users):
        for k in range(HEADS):
            split_ref[k // CORES, u, k % CORES] = pool_ref[slots[u], :, :, k * hd : (k + 1) * hd]
        copies.append(pltpu.make_async_copy(split_ref.at[:, u], out_ref.at[:, u], sems.at[u]))
        copies[-1].start()
    for copy in copies:
        copy.wait()


def split_pages(told, kv_pool):
    _, _, page, width = kv_pool.shape
    shape = (HEADS // CORES, told.shape[0], CORES, 2, page, width // HEADS)
    return pl.pallas_call(
        split_pages_kernel,
        in_specs=[SMEM, VMEM],
        out_specs=HBM,
        out_shape=jax.ShapeDtypeStruct(shape, kv_pool.dtype),
        scratch_shapes=[pltpu.VMEM(shape, kv_pool.dtype), pltpu.SemaphoreType.DMA((told.shape[0],))],
        name="split_pages",
    )(told, kv_pool)


STEPS = (0, -1, 1, -3, -2, 3, 4, 2)


def gather_queries(row):
    below, above = shift(row, "y", 1), shift(row, "y", -1)
    below3 = shift(jnp.concatenate([row, above]), "y", 3)
    above3 = shift(jnp.concatenate([row, above, below]), "y", -3)
    return below, above, below3, above3


def attend_kernel(scale, info_ref, row_ref, kv_ref, *rest):
    pieces, (out_ref, q_ref, acc_ref) = rest[:-3], rest[-3:]
    n_x, n_y, cores, rows, hd = out_ref.shape
    sources, tiles = n_x * cores, len(STEPS)
    span = sources * PAGE
    height = n_x * cores * rows
    y = lax.axis_index("y")
    blocks = [row_ref[...]]
    for piece in pieces:
        blocks += [piece[b * height : (b + 1) * height, :] for b in range(piece.shape[0] // height)]
    for step, block in zip(STEPS, blocks):
        q_ref[pl.ds(lax.rem(y + (step + tiles), tiles) * height, height), :] = block
    place = lax.broadcasted_iota(jnp.int32, (sources, span), 1)
    which = lax.broadcasted_iota(jnp.int32, (sources, span), 0)
    spread = (place // PAGE == which).astype(jnp.bfloat16)
    fields = lax.dot_general(
        info_ref[...], spread, (((0,), (0,)), ((), ())), preferred_element_type=jnp.float32
    )
    within = lax.rem(lax.broadcasted_iota(jnp.int32, (1, span), 1), PAGE).astype(jnp.float32)
    q = q_ref[...]
    for o in range(kv_ref.shape[1]):
        keys = kv_ref[:, o, :, 0].reshape(span, hd)
        values = kv_ref[:, o, :, 1].reshape(span, hd)
        seen = fields[o * FIELDS : o * FIELDS + tiles]
        live = fields[o * FIELDS + LIVE : o * FIELDS + LIVE + 1]
        allowed = jnp.where(within < live, seen, 0.0).astype(jnp.bfloat16)
        score = lax.dot_general(q, keys, (((1,), (1,)), ((), ())), preferred_element_type=jnp.float32)
        weight = silu(score * scale).astype(jnp.bfloat16)
        weight = weight.reshape(tiles, height, span) * allowed[:, None, :]
        part = jnp.dot(weight.reshape(tiles * height, span), values, preferred_element_type=jnp.float32)
        if o == 0:
            acc_ref[...] = part
        else:
            acc_ref[...] += part
    total = acc_ref[...].astype(out_ref.dtype).reshape(n_y, n_x, cores, rows, hd)
    for t in range(n_y):
        out_ref[:, t] = total[t]


def attend(info, row, pages, pieces, scale):
    n_x, _, cores, _, _, hd = pages.shape
    rows = row.shape[0] // (n_x * cores)
    out = jax.ShapeDtypeStruct((n_x, len(STEPS), cores, rows, hd), jnp.bfloat16)
    height = out.size // hd
    return pl.pallas_call(
        functools.partial(attend_kernel, scale),
        in_specs=[VMEM] * (3 + len(pieces)),
        out_specs=VMEM,
        out_shape=out,
        scratch_shapes=[pltpu.VMEM((height, hd), jnp.bfloat16), pltpu.VMEM((height, hd), jnp.float32)],
        compiler_params=pltpu.CompilerParams(vmem_limit_bytes=16 * 1024 * 1024),
        name="attend",
    )(info, row, pages, *pieces)


def finish_kernel(back_ref, own_ref, u_ref, gain_ref, input_ref, weight_ref, out_ref):
    attn = []
    for h in range(HEADS):
        total = back_ref[h // CORES, 0, h % CORES].astype(jnp.float32)
        for y in range(1, back_ref.shape[1]):
            total += back_ref[h // CORES, y, h % CORES].astype(jnp.float32)
        attn.append(total)
    attn = jnp.concatenate(attn, axis=1) + own_ref[...]
    mean = jnp.mean(attn, axis=1, keepdims=True)
    centered = attn - mean
    var = jnp.mean(centered * centered, axis=1, keepdims=True)
    gate = gain_ref[...] * u_ref[...].astype(jnp.float32)
    normed = (centered * lax.rsqrt(var + eps) * gate).astype(jnp.bfloat16)
    out = jnp.dot(normed, weight_ref[...], preferred_element_type=jnp.float32)
    out_ref[...] = (input_ref[...].astype(jnp.float32) + out).astype(out_ref.dtype)


def finish(back, own, u_act, out_gain, cand_input, out_weight):
    return pl.pallas_call(
        finish_kernel,
        in_specs=[VMEM] * 6,
        out_specs=VMEM,
        out_shape=jax.ShapeDtypeStruct(cand_input.shape, cand_input.dtype),
        compiler_params=pltpu.CompilerParams(vmem_limit_bytes=16 * 1024 * 1024),
        name="finish",
    )(back, own, u_act, out_gain.reshape(1, -1), cand_input, out_weight)


def on_device(
    cand_proj, cand_input, kv_pool, page_owner, page_slot, lengths, block_mask, out_gain, out_weight
):
    rows, width = cand_input.shape
    hd = width // HEADS
    scale = hd ** (-0.5)
    n_z = lax.axis_size("z")
    owners = page_owner.reshape(-1)

    places = page_owner * kv_pool.shape[0] + page_slot
    told = exchange(jnp.broadcast_to(places, (n_z,) + places.shape[1:]), ("z",))
    asked, own, u_act = ask(owners, lengths, block_mask[0].T, cand_proj, scale)
    told, asked = lax.optimization_barrier((told, asked))
    asked = exchange(asked, ("x", "c"))
    pages = split_pages(told.reshape(n_z, -1), kv_pool)
    pages, asked = lax.optimization_barrier((pages, asked))
    got = exchange(pages.reshape((-1,) + pages.shape[3:]), PAGES).reshape(pages.shape)
    row, info = asked[:, :rows].reshape(-1, hd), asked[:, rows]
    part = attend(info, row, got, gather_queries(row), scale)
    back = exchange(part.reshape(-1, rows, hd), SUMS).reshape(part.shape)
    return finish(back, own, u_act, out_gain, cand_input, out_weight)


def solution(mesh):
    n_z, n_p = mesh.shape["batch"], mesh.shape["pos"]
    n_x = HEADS // CORES
    grid = Mesh(mesh.devices.reshape(n_z, n_p // HEADS, n_x, CORES), ("z", "y", "x", "c"))
    rows = P(("z", "y", "x", "c"), None)
    placed = (
        rows,
        rows,
        P("z", None, PLANE, None),
        P("z", PLANE, None),
        P("z", PLANE, None),
        P("z"),
        P("z", None, PLANE),
        P(),
        P(),
    )
    return jax.shard_map(on_device, mesh=grid, in_specs=placed, out_specs=rows, check_vma=False)
```

```python
import functools

import jax
import jax.numpy as jnp
from jax import lax
from jax.experimental import pallas as pl
from jax.experimental.pallas import tpu as pltpu
from jax.sharding import Mesh
from jax.sharding import PartitionSpec as P

HEADS = 8
PAGE = 32
eps = 1e-05

PLANE = ("y", "x", "c")
SPREAD = ("z", "x", "c")
PAGES = ("x", "z", "c")
SUMS = ("x", "y", "c")
CORES = 2

FIELDS = 16
LIVE = 8

VMEM = pl.BlockSpec(memory_space=pltpu.VMEM)
SMEM = pl.BlockSpec(memory_space=pltpu.SMEM)
HBM = pl.BlockSpec(memory_space=pl.ANY)


def exchange(array, axes):
    return lax.all_to_all(array, axes, split_axis=0, concat_axis=0, tiled=True)


def shift(array, axis, step):
    n = lax.axis_size(axis)
    return lax.ppermute(array, axis, [(i, (i + step) % n) for i in range(n)])


def silu(value):
    half = value * 0.5
    return half + half * jnp.tanh(half)


def ask_kernel(scale, owner_ref, length_ref, seen_ref, proj_ref, out_ref, own_ref, u_ref):
    pages = owner_ref.shape[0]
    blocks, tiles = seen_ref.shape
    rows, hd = out_ref.shape[1] // 2, out_ref.shape[2]
    place = lax.axis_index(PLANE)
    lane = lax.broadcasted_iota(jnp.int32, (rows, hd), 1)
    owner, field = lane // FIELDS, lane % FIELDS
    seen = []
    for b in range(blocks):
        row = jnp.zeros((rows, hd), jnp.int32)
        for t in range(tiles):
            row = jnp.where(field == t, seen_ref[b : b + 1, t : t + 1], row)
        seen.append(row)
    info = jnp.zeros((rows, hd), jnp.int32)
    for j in range(pages):
        live = jnp.clip(length_ref[0] - (place * pages + j) * PAGE, 0, PAGE)
        row = jnp.where(field == LIVE, live, seen[j * blocks // pages])
        info = jnp.where(owner == owner_ref[j], row, info)
    info = info.astype(jnp.float32).astype(jnp.bfloat16)

    def act(block, h):
        start = (block * HEADS + h) * hd
        return silu(proj_ref[:, start : start + hd].astype(jnp.float32)).astype(jnp.bfloat16)

    for h in range(HEADS):
        part = slice(h * hd, (h + 1) * hd)
        query = act(2, h)
        out_ref[h, :rows] = query
        out_ref[h, rows:] = info
        score = query.astype(jnp.float32) * act(3, h).astype(jnp.float32)
        own = silu(jnp.sum(score, axis=1, keepdims=True) * scale).astype(jnp.bfloat16)
        own_ref[:, part] = own.astype(jnp.float32) * act(1, h).astype(jnp.float32)
        u_ref[:, part] = act(0, h)


def ask(owners, lengths, seen, cand_proj, scale):
    rows, width = cand_proj.shape[0], cand_proj.shape[1] // 4
    hd = width // HEADS
    return pl.pallas_call(
        functools.partial(ask_kernel, scale),
        in_specs=[SMEM] * 2 + [VMEM] * 2,
        out_specs=[VMEM] * 3,
        out_shape=[
            jax.ShapeDtypeStruct((HEADS, 2 * rows, hd), jnp.bfloat16),
            jax.ShapeDtypeStruct((rows, width), jnp.float32),
            jax.ShapeDtypeStruct((rows, width), jnp.bfloat16),
        ],
        name="ask",
    )(owners, lengths, seen, cand_proj)


def split_pages_kernel(told_ref, pool_ref, out_ref, split_ref, sems):
    n_x, users = out_ref.shape[:2]
    hd = out_ref.shape[5]
    count = pool_ref.shape[0]
    first = lax.axis_index("z") * count
    slots = []
    for u in range(users):
        slot = jnp.int32(0)
        for j in range(told_ref.shape[1]):
            at = told_ref[u, j] - first
            slot = jnp.where((at >= 0) & (at < count), at, slot)
        slots.append(slot)
    copies = []
    for u in range(users):
        for k in range(HEADS):
            split_ref[k // CORES, u, k % CORES] = pool_ref[slots[u], :, :, k * hd : (k + 1) * hd]
        copies.append(pltpu.make_async_copy(split_ref.at[:, u], out_ref.at[:, u], sems.at[u]))
        copies[-1].start()
    for copy in copies:
        copy.wait()


def split_pages(told, kv_pool):
    _, _, page, width = kv_pool.shape
    shape = (HEADS // CORES, told.shape[0], CORES, 2, page, width // HEADS)
    return pl.pallas_call(
        split_pages_kernel,
        in_specs=[SMEM, VMEM],
        out_specs=HBM,
        out_shape=jax.ShapeDtypeStruct(shape, kv_pool.dtype),
        scratch_shapes=[pltpu.VMEM(shape, kv_pool.dtype), pltpu.SemaphoreType.DMA((told.shape[0],))],
        name="split_pages",
    )(told, kv_pool)


STEPS = (0, -1, 1, -3, -2, 3, 4, 2)


def gather_queries(row):
    below, above = shift(row, "y", 1), shift(row, "y", -1)
    below3 = shift(jnp.concatenate([row, above]), "y", 3)
    above3 = shift(jnp.concatenate([row, above, below]), "y", -3)
    return below, above, below3, above3


def attend_kernel(scale, info_ref, row_ref, kv_ref, *rest):
    pieces, (out_ref, q_ref, acc_ref) = rest[:-3], rest[-3:]
    n_x, n_y, cores, rows, hd = out_ref.shape
    sources, tiles = n_x * cores, len(STEPS)
    span = sources * PAGE
    height = n_x * cores * rows
    y = lax.axis_index("y")
    blocks = [row_ref[...]]
    for piece in pieces:
        blocks += [piece[b * height : (b + 1) * height, :] for b in range(piece.shape[0] // height)]
    for step, block in zip(STEPS, blocks):
        start = pl.multiple_of(lax.rem(y + (step + tiles), tiles) * height, height)
        q_ref[pl.ds(start, height), :] = block
    place = lax.broadcasted_iota(jnp.int32, (sources, span), 1)
    which = lax.broadcasted_iota(jnp.int32, (sources, span), 0)
    spread = (place // PAGE == which).astype(jnp.bfloat16)
    fields = lax.dot_general(
        info_ref[...].astype(jnp.bfloat16), spread, (((0,), (0,)), ((), ())), preferred_element_type=jnp.float32
    )
    within = lax.rem(lax.broadcasted_iota(jnp.int32, (1, span), 1), PAGE).astype(jnp.float32)
    q = q_ref[...]
    for o in range(kv_ref.shape[1]):
        keys = kv_ref[:, o, :, 0].reshape(span, hd)
        values = kv_ref[:, o, :, 1].reshape(span, hd)
        seen = fields[o * FIELDS : o * FIELDS + tiles]
        live = fields[o * FIELDS + LIVE : o * FIELDS + LIVE + 1]
        allowed = jnp.where(within < live, seen, 0.0).astype(jnp.bfloat16)
        score = lax.dot_general(q, keys, (((1,), (1,)), ((), ())), preferred_element_type=jnp.float32)
        weight = silu(score * scale).astype(jnp.bfloat16)
        weight = weight.reshape(tiles, height, span) * allowed[:, None, :]
        part = jnp.dot(weight.reshape(tiles * height, span), values, preferred_element_type=jnp.float32)
        if o == 0:
            acc_ref[...] = part
        else:
            acc_ref[...] += part
    total = acc_ref[...].astype(out_ref.dtype).reshape(n_y, n_x, cores, rows, hd)
    for t in range(n_y):
        out_ref[:, t] = total[t]


def attend(info, row, pages, pieces, scale):
    n_x, _, cores, _, _, hd = pages.shape
    rows = row.shape[0] // (n_x * cores)
    out = jax.ShapeDtypeStruct((n_x, len(STEPS), cores, rows, hd), jnp.bfloat16)
    height = out.size // hd
    return pl.pallas_call(
        functools.partial(attend_kernel, scale),
        in_specs=[VMEM] * (3 + len(pieces)),
        out_specs=VMEM,
        out_shape=out,
        scratch_shapes=[pltpu.VMEM((height, hd), jnp.bfloat16), pltpu.VMEM((height, hd), jnp.float32)],
        compiler_params=pltpu.CompilerParams(vmem_limit_bytes=16 * 1024 * 1024),
        name="attend",
    )(info, row, pages, *pieces)


def finish_kernel(back_ref, own_ref, u_ref, gain_ref, input_ref, weight_ref, out_ref):
    attn = []
    for h in range(HEADS):
        total = back_ref[h // CORES, 0, h % CORES].astype(jnp.float32)
        for y in range(1, back_ref.shape[1]):
            total += back_ref[h // CORES, y, h % CORES].astype(jnp.float32)
        attn.append(total)
    attn = jnp.concatenate(attn, axis=1) + own_ref[...]
    mean = jnp.mean(attn, axis=1, keepdims=True)
    centered = attn - mean
    var = jnp.mean(centered * centered, axis=1, keepdims=True)
    gate = gain_ref[...] * u_ref[...].astype(jnp.float32)
    normed = (centered * lax.rsqrt(var + eps) * gate).astype(jnp.bfloat16)
    out = jnp.dot(normed, weight_ref[...], preferred_element_type=jnp.float32)
    out_ref[...] = (input_ref[...].astype(jnp.float32) + out).astype(out_ref.dtype)


def finish(back, own, u_act, out_gain, cand_input, out_weight):
    return pl.pallas_call(
        finish_kernel,
        in_specs=[VMEM] * 6,
        out_specs=VMEM,
        out_shape=jax.ShapeDtypeStruct(cand_input.shape, cand_input.dtype),
        compiler_params=pltpu.CompilerParams(vmem_limit_bytes=16 * 1024 * 1024),
        name="finish",
    )(back, own, u_act, out_gain.reshape(1, -1), cand_input, out_weight)


def on_device(
    cand_proj, cand_input, kv_pool, page_owner, page_slot, lengths, block_mask, out_gain, out_weight
):
    rows, width = cand_input.shape
    hd = width // HEADS
    scale = hd ** (-0.5)
    n_z = lax.axis_size("z")
    owners = page_owner.reshape(-1)

    places = page_owner * kv_pool.shape[0] + page_slot
    told = exchange(jnp.broadcast_to(places, (n_z,) + places.shape[1:]), ("z",))
    asked, own, u_act = ask(owners, lengths, block_mask[0].T, cand_proj, scale)
    told, asked = lax.optimization_barrier((told, asked))
    asked = exchange(asked, ("x", "c"))
    pages = split_pages(told.reshape(n_z, -1), kv_pool)
    pages, asked = lax.optimization_barrier((pages, asked))
    got = exchange(pages.reshape((-1,) + pages.shape[3:]), PAGES).reshape(pages.shape)
    row, info = asked[:, :rows].reshape(-1, hd), asked[:, rows].astype(jnp.float32)
    part = attend(info, row, got, gather_queries(row), scale)
    back = exchange(part.reshape(-1, rows, hd), SUMS).reshape(part.shape)
    return finish(back, own, u_act, out_gain, cand_input, out_weight)


def solution(mesh):
    n_z, n_p = mesh.shape["batch"], mesh.shape["pos"]
    n_x = HEADS // CORES
    grid = Mesh(mesh.devices.reshape(n_z, n_p // HEADS, n_x, CORES), ("z", "y", "x", "c"))
    rows = P(("z", "y", "x", "c"), None)
    placed = (
        rows,
        rows,
        P("z", None, PLANE, None),
        P("z", PLANE, None),
        P("z", PLANE, None),
        P("z"),
        P("z", None, PLANE),
        P(),
        P(),
    )
    return jax.shard_map(on_device, mesh=grid, in_specs=placed, out_specs=rows, check_vma=False)
```

```python
import functools

import jax
import jax.numpy as jnp
from jax import lax
from jax.experimental import pallas as pl
from jax.experimental.pallas import tpu as pltpu
from jax.sharding import Mesh
from jax.sharding import PartitionSpec as P

HEADS = 8
PAGE = 32
eps = 1e-05

PLANE = ("y", "x", "c")
SPREAD = ("z", "x", "c")
PAGES = ("x", "z", "c")
SUMS = ("x", "c", "y")
CORES = 2

FIELDS = 16
LIVE = 8

VMEM = pl.BlockSpec(memory_space=pltpu.VMEM)
SMEM = pl.BlockSpec(memory_space=pltpu.SMEM)
HBM = pl.BlockSpec(memory_space=pl.ANY)


def exchange(array, axes):
    return lax.all_to_all(array, axes, split_axis=0, concat_axis=0, tiled=True)


def shift(array, axis, step):
    n = lax.axis_size(axis)
    return lax.ppermute(array, axis, [(i, (i + step) % n) for i in range(n)])


def silu(value):
    half = value * 0.5
    return half + half * jnp.tanh(half)


def ask_kernel(scale, owner_ref, length_ref, seen_ref, proj_ref, out_ref, own_ref, u_ref):
    pages = owner_ref.shape[0]
    blocks, tiles = seen_ref.shape
    rows, hd = out_ref.shape[1] // 2, out_ref.shape[2]
    place = lax.axis_index(PLANE)
    lane = lax.broadcasted_iota(jnp.int32, (rows, hd), 1)
    owner, field = lane // FIELDS, lane % FIELDS
    seen = []
    for b in range(blocks):
        row = jnp.zeros((rows, hd), jnp.int32)
        for t in range(tiles):
            row = jnp.where(field == t, seen_ref[b : b + 1, t : t + 1], row)
        seen.append(row)
    info = jnp.zeros((rows, hd), jnp.int32)
    for j in range(pages):
        live = jnp.clip(length_ref[0] - (place * pages + j) * PAGE, 0, PAGE)
        row = jnp.where(field == LIVE, live, seen[j * blocks // pages])
        info = jnp.where(owner == owner_ref[j], row, info)
    info = info.astype(jnp.float32).astype(jnp.bfloat16)

    def act(block, h):
        start = (block * HEADS + h) * hd
        return silu(proj_ref[:, start : start + hd].astype(jnp.float32)).astype(jnp.bfloat16)

    for h in range(HEADS):
        part = slice(h * hd, (h + 1) * hd)
        query = act(2, h)
        out_ref[h, :rows] = query
        out_ref[h, rows:] = info
        score = query.astype(jnp.float32) * act(3, h).astype(jnp.float32)
        own = silu(jnp.sum(score, axis=1, keepdims=True) * scale).astype(jnp.bfloat16)
        own_ref[:, part] = own.astype(jnp.float32) * act(1, h).astype(jnp.float32)
        u_ref[:, part] = act(0, h)


def ask(owners, lengths, seen, cand_proj, scale):
    rows, width = cand_proj.shape[0], cand_proj.shape[1] // 4
    hd = width // HEADS
    return pl.pallas_call(
        functools.partial(ask_kernel, scale),
        in_specs=[SMEM] * 2 + [VMEM] * 2,
        out_specs=[VMEM] * 3,
        out_shape=[
            jax.ShapeDtypeStruct((HEADS, 2 * rows, hd), jnp.bfloat16),
            jax.ShapeDtypeStruct((rows, width), jnp.float32),
            jax.ShapeDtypeStruct((rows, width), jnp.bfloat16),
        ],
        name="ask",
    )(owners, lengths, seen, cand_proj)


def split_pages_kernel(told_ref, pool_ref, out_ref, split_ref, sems):
    n_x, users = out_ref.shape[:2]
    hd = out_ref.shape[5]
    count = pool_ref.shape[0]
    first = lax.axis_index("z") * count
    slots = []
    for u in range(users):
        slot = jnp.int32(0)
        for j in range(told_ref.shape[1]):
            at = told_ref[u, j] - first
            slot = jnp.where((at >= 0) & (at < count), at, slot)
        slots.append(slot)
    copies = []
    for u in range(users):
        for k in range(HEADS):
            split_ref[k // CORES, u, k % CORES] = pool_ref[slots[u], :, :, k * hd : (k + 1) * hd]
        copies.append(pltpu.make_async_copy(split_ref.at[:, u], out_ref.at[:, u], sems.at[u]))
        copies[-1].start()
    for copy in copies:
        copy.wait()


def split_pages(told, kv_pool):
    _, _, page, width = kv_pool.shape
    shape = (HEADS // CORES, told.shape[0], CORES, 2, page, width // HEADS)
    return pl.pallas_call(
        split_pages_kernel,
        in_specs=[SMEM, VMEM],
        out_specs=HBM,
        out_shape=jax.ShapeDtypeStruct(shape, kv_pool.dtype),
        scratch_shapes=[pltpu.VMEM(shape, kv_pool.dtype), pltpu.SemaphoreType.DMA((told.shape[0],))],
        name="split_pages",
    )(told, kv_pool)


STEPS = (0, -1, 1, -3, -2, 3, 4, 2)


def gather_queries(row):
    below, above = shift(row, "y", 1), shift(row, "y", -1)
    below3 = shift(jnp.concatenate([row, above]), "y", 3)
    above3 = shift(jnp.concatenate([row, above, below]), "y", -3)
    return below, above, below3, above3


def attend_kernel(scale, info_ref, row_ref, kv_ref, *rest):
    pieces, (out_ref, q_ref, acc_ref) = rest[:-3], rest[-3:]
    n_x, cores, n_y, rows, hd = out_ref.shape
    sources, tiles = n_x * cores, len(STEPS)
    span = sources * PAGE
    height = n_x * cores * rows
    y = lax.axis_index("y")
    blocks = [row_ref[...]]
    for piece in pieces:
        blocks += [piece[b * height : (b + 1) * height, :] for b in range(piece.shape[0] // height)]
    for step, block in zip(STEPS, blocks):
        start = pl.multiple_of(lax.rem(y + (step + tiles), tiles) * height, height)
        q_ref[pl.ds(start, height), :] = block
    place = lax.broadcasted_iota(jnp.int32, (sources, span), 1)
    which = lax.broadcasted_iota(jnp.int32, (sources, span), 0)
    spread = (place // PAGE == which).astype(jnp.bfloat16)
    fields = lax.dot_general(
        info_ref[...].astype(jnp.bfloat16), spread, (((0,), (0,)), ((), ())), preferred_element_type=jnp.float32
    )
    within = lax.rem(lax.broadcasted_iota(jnp.int32, (1, span), 1), PAGE).astype(jnp.float32)
    q = q_ref[...]
    for o in range(kv_ref.shape[1]):
        keys = kv_ref[:, o, :, 0].reshape(span, hd)
        values = kv_ref[:, o, :, 1].reshape(span, hd)
        seen = fields[o * FIELDS : o * FIELDS + tiles]
        live = fields[o * FIELDS + LIVE : o * FIELDS + LIVE + 1]
        allowed = jnp.where(within < live, seen, 0.0).astype(jnp.bfloat16)
        score = lax.dot_general(q, keys, (((1,), (1,)), ((), ())), preferred_element_type=jnp.float32)
        weight = silu(score * scale).astype(jnp.bfloat16)
        weight = weight.reshape(tiles, height, span) * allowed[:, None, :]
        part = jnp.dot(weight.reshape(tiles * height, span), values, preferred_element_type=jnp.float32)
        if o == 0:
            acc_ref[...] = part
        else:
            acc_ref[...] += part
    total = acc_ref[...].astype(out_ref.dtype).reshape(n_y, n_x, cores, rows, hd)
    for t in range(n_y):
        out_ref[:, :, t] = total[t]


def attend(info, row, pages, pieces, scale):
    n_x, _, cores, _, _, hd = pages.shape
    rows = row.shape[0] // (n_x * cores)
    out = jax.ShapeDtypeStruct((n_x, cores, len(STEPS), rows, hd), jnp.bfloat16)
    height = out.size // hd
    return pl.pallas_call(
        functools.partial(attend_kernel, scale),
        in_specs=[VMEM] * (3 + len(pieces)),
        out_specs=VMEM,
        out_shape=out,
        scratch_shapes=[pltpu.VMEM((height, hd), jnp.bfloat16), pltpu.VMEM((height, hd), jnp.float32)],
        compiler_params=pltpu.CompilerParams(vmem_limit_bytes=16 * 1024 * 1024),
        name="attend",
    )(info, row, pages, *pieces)


def finish_kernel(back_ref, own_ref, u_ref, gain_ref, input_ref, weight_ref, out_ref):
    attn = []
    for h in range(HEADS):
        total = back_ref[h // CORES, h % CORES, 0].astype(jnp.float32)
        for y in range(1, back_ref.shape[2]):
            total += back_ref[h // CORES, h % CORES, y].astype(jnp.float32)
        attn.append(total)
    attn = jnp.concatenate(attn, axis=1) + own_ref[...]
    mean = jnp.mean(attn, axis=1, keepdims=True)
    centered = attn - mean
    var = jnp.mean(centered * centered, axis=1, keepdims=True)
    gate = gain_ref[...] * u_ref[...].astype(jnp.float32)
    normed = (centered * lax.rsqrt(var + eps) * gate).astype(jnp.bfloat16)
    out = jnp.dot(normed, weight_ref[...], preferred_element_type=jnp.float32)
    out_ref[...] = (input_ref[...].astype(jnp.float32) + out).astype(out_ref.dtype)


def finish(back, own, u_act, out_gain, cand_input, out_weight):
    return pl.pallas_call(
        finish_kernel,
        in_specs=[VMEM] * 6,
        out_specs=VMEM,
        out_shape=jax.ShapeDtypeStruct(cand_input.shape, cand_input.dtype),
        compiler_params=pltpu.CompilerParams(vmem_limit_bytes=16 * 1024 * 1024),
        name="finish",
    )(back, own, u_act, out_gain.reshape(1, -1), cand_input, out_weight)


def on_device(
    cand_proj, cand_input, kv_pool, page_owner, page_slot, lengths, block_mask, out_gain, out_weight
):
    rows, width = cand_input.shape
    hd = width // HEADS
    scale = hd ** (-0.5)
    n_z = lax.axis_size("z")
    owners = page_owner.reshape(-1)

    places = page_owner * kv_pool.shape[0] + page_slot
    told = exchange(jnp.broadcast_to(places, (n_z,) + places.shape[1:]), ("z",))
    asked, own, u_act = ask(owners, lengths, block_mask[0].T, cand_proj, scale)
    told, asked = lax.optimization_barrier((told, asked))
    asked = exchange(asked, ("x", "c"))
    pages = split_pages(told.reshape(n_z, -1), kv_pool)
    _, asked = lax.optimization_barrier((pages, asked))
    got = exchange(pages.reshape((-1,) + pages.shape[3:]), PAGES).reshape(pages.shape)
    row, info = asked[:, :rows].reshape(-1, hd), asked[:, rows].astype(jnp.float32)
    part = attend(info, row, got, gather_queries(row), scale)
    back = exchange(part.reshape(-1, rows, hd), SUMS).reshape(part.shape)
    return finish(back, own, u_act, out_gain, cand_input, out_weight)


def solution(mesh):
    n_z, n_p = mesh.shape["batch"], mesh.shape["pos"]
    n_x = HEADS // CORES
    grid = Mesh(mesh.devices.reshape(n_z, n_p // HEADS, n_x, CORES), ("z", "y", "x", "c"))
    rows = P(("z", "y", "x", "c"), None)
    placed = (
        rows,
        rows,
        P("z", None, PLANE, None),
        P("z", PLANE, None),
        P("z", PLANE, None),
        P("z"),
        P("z", None, PLANE),
        P(),
        P(),
    )
    return jax.shard_map(on_device, mesh=grid, in_specs=placed, out_specs=rows, check_vma=False)
```

```python
import functools

import jax
import jax.numpy as jnp
from jax import lax
from jax.experimental import pallas as pl
from jax.experimental.pallas import tpu as pltpu
from jax.sharding import Mesh
from jax.sharding import PartitionSpec as P

HEADS = 8
PAGE = 32
eps = 1e-05

PLANE = ("y", "x", "c")
SPREAD = ("z", "x", "c")
PAGES = ("x", "z", "c")
SUMS = ("x", "c", "y")
CORES = 2

FIELDS = 16
LIVE = 8

VMEM = pl.BlockSpec(memory_space=pltpu.VMEM)
SMEM = pl.BlockSpec(memory_space=pltpu.SMEM)
HBM = pl.BlockSpec(memory_space=pl.ANY)


def exchange(array, axes):
    return lax.all_to_all(array, axes, split_axis=0, concat_axis=0, tiled=True)


def shift(array, axis, step):
    n = lax.axis_size(axis)
    return lax.ppermute(array, axis, [(i, (i + step) % n) for i in range(n)])


def silu(value):
    return value / (1.0 + jnp.exp(-value))


def ask_kernel(scale, owner_ref, length_ref, seen_ref, proj_ref, out_ref, own_ref, u_ref):
    pages = owner_ref.shape[0]
    blocks, tiles = seen_ref.shape
    rows, hd = out_ref.shape[1] // 2, out_ref.shape[2]
    place = lax.axis_index(PLANE)
    lane = lax.broadcasted_iota(jnp.int32, (rows, hd), 1)
    owner, field = lane // FIELDS, lane % FIELDS
    seen = []
    for b in range(blocks):
        row = jnp.zeros((rows, hd), jnp.int32)
        for t in range(tiles):
            row = jnp.where(field == t, seen_ref[b : b + 1, t : t + 1], row)
        seen.append(row)
    info = jnp.zeros((rows, hd), jnp.int32)
    for j in range(pages):
        live = jnp.clip(length_ref[0] - (place * pages + j) * PAGE, 0, PAGE)
        row = jnp.where(field == LIVE, live, seen[j * blocks // pages])
        info = jnp.where(owner == owner_ref[j], row, info)
    info = info.astype(jnp.float32).astype(jnp.bfloat16)

    def act(block, h):
        start = (block * HEADS + h) * hd
        return silu(proj_ref[:, start : start + hd].astype(jnp.float32)).astype(jnp.bfloat16)

    for h in range(HEADS):
        part = slice(h * hd, (h + 1) * hd)
        query = act(2, h)
        out_ref[h, :rows] = query
        out_ref[h, rows:] = info
        score = query.astype(jnp.float32) * act(3, h).astype(jnp.float32)
        own = silu(jnp.sum(score, axis=1, keepdims=True) * scale).astype(jnp.bfloat16)
        own_ref[:, part] = own.astype(jnp.float32) * act(1, h).astype(jnp.float32)
        u_ref[:, part] = act(0, h)


def ask(owners, lengths, seen, cand_proj, scale):
    rows, width = cand_proj.shape[0], cand_proj.shape[1] // 4
    hd = width // HEADS
    return pl.pallas_call(
        functools.partial(ask_kernel, scale),
        in_specs=[SMEM] * 2 + [VMEM] * 2,
        out_specs=[VMEM] * 3,
        out_shape=[
            jax.ShapeDtypeStruct((HEADS, 2 * rows, hd), jnp.bfloat16),
            jax.ShapeDtypeStruct((rows, width), jnp.float32),
            jax.ShapeDtypeStruct((rows, width), jnp.bfloat16),
        ],
        name="ask",
    )(owners, lengths, seen, cand_proj)


def split_pages_kernel(told_ref, pool_ref, out_ref, split_ref, sems):
    n_x, users = out_ref.shape[:2]
    hd = out_ref.shape[5]
    count = pool_ref.shape[0]
    first = lax.axis_index("z") * count
    slots = []
    for u in range(users):
        slot = jnp.int32(0)
        for j in range(told_ref.shape[1]):
            at = told_ref[u, j] - first
            slot = jnp.where((at >= 0) & (at < count), at, slot)
        slots.append(slot)
    copies = []
    for u in range(users):
        for k in range(HEADS):
            split_ref[k // CORES, u, k % CORES] = pool_ref[slots[u], :, :, k * hd : (k + 1) * hd]
        copies.append(pltpu.make_async_copy(split_ref.at[:, u], out_ref.at[:, u], sems.at[u]))
        copies[-1].start()
    for copy in copies:
        copy.wait()


def split_pages(told, kv_pool):
    _, _, page, width = kv_pool.shape
    shape = (HEADS // CORES, told.shape[0], CORES, 2, page, width // HEADS)
    return pl.pallas_call(
        split_pages_kernel,
        in_specs=[SMEM, VMEM],
        out_specs=HBM,
        out_shape=jax.ShapeDtypeStruct(shape, kv_pool.dtype),
        scratch_shapes=[pltpu.VMEM(shape, kv_pool.dtype), pltpu.SemaphoreType.DMA((told.shape[0],))],
        name="split_pages",
    )(told, kv_pool)


STEPS = (0, -1, 1, -3, -2, 3, 4, 2)


def gather_queries(row):
    below, above = shift(row, "y", 1), shift(row, "y", -1)
    below3 = shift(jnp.concatenate([row, above]), "y", 3)
    above3 = shift(jnp.concatenate([row, above, below]), "y", -3)
    return below, above, below3, above3


def attend_kernel(scale, info_ref, row_ref, kv_ref, *rest):
    pieces, (out_ref, q_ref, acc_ref) = rest[:-3], rest[-3:]
    n_x, cores, n_y, rows, hd = out_ref.shape
    sources, tiles = n_x * cores, len(STEPS)
    span = sources * PAGE
    height = n_x * cores * rows
    y = lax.axis_index("y")
    blocks = [row_ref[...]]
    for piece in pieces:
        blocks += [piece[b * height : (b + 1) * height, :] for b in range(piece.shape[0] // height)]
    for step, block in zip(STEPS, blocks):
        start = pl.multiple_of(lax.rem(y + (step + tiles), tiles) * height, height)
        q_ref[pl.ds(start, height), :] = block
    place = lax.broadcasted_iota(jnp.int32, (sources, span), 1)
    which = lax.broadcasted_iota(jnp.int32, (sources, span), 0)
    spread = (place // PAGE == which).astype(jnp.bfloat16)
    fields = lax.dot_general(
        info_ref[...].astype(jnp.bfloat16), spread, (((0,), (0,)), ((), ())), preferred_element_type=jnp.float32
    )
    within = lax.rem(lax.broadcasted_iota(jnp.int32, (1, span), 1), PAGE).astype(jnp.float32)
    q = q_ref[...]
    for o in range(kv_ref.shape[1]):
        keys = kv_ref[:, o, :, 0].reshape(span, hd)
        values = kv_ref[:, o, :, 1].reshape(span, hd)
        seen = fields[o * FIELDS : o * FIELDS + tiles]
        live = fields[o * FIELDS + LIVE : o * FIELDS + LIVE + 1]
        allowed = jnp.where(within < live, seen, 0.0).astype(jnp.bfloat16)
        score = lax.dot_general(q, keys, (((1,), (1,)), ((), ())), preferred_element_type=jnp.float32)
        weight = silu(score * scale).astype(jnp.bfloat16)
        weight = weight.reshape(tiles, height, span) * allowed[:, None, :]
        part = jnp.dot(weight.reshape(tiles * height, span), values, preferred_element_type=jnp.float32)
        if o == 0:
            acc_ref[...] = part
        else:
            acc_ref[...] += part
    total = acc_ref[...].astype(out_ref.dtype).reshape(n_y, n_x, cores, rows, hd)
    for t in range(n_y):
        out_ref[:, :, t] = total[t]


def attend(info, row, pages, pieces, scale):
    n_x, _, cores, _, _, hd = pages.shape
    rows = row.shape[0] // (n_x * cores)
    out = jax.ShapeDtypeStruct((n_x, cores, len(STEPS), rows, hd), jnp.bfloat16)
    height = out.size // hd
    return pl.pallas_call(
        functools.partial(attend_kernel, scale),
        in_specs=[VMEM] * (3 + len(pieces)),
        out_specs=VMEM,
        out_shape=out,
        scratch_shapes=[pltpu.VMEM((height, hd), jnp.bfloat16), pltpu.VMEM((height, hd), jnp.float32)],
        compiler_params=pltpu.CompilerParams(vmem_limit_bytes=16 * 1024 * 1024),
        name="attend",
    )(info, row, pages, *pieces)


def finish_kernel(back_ref, own_ref, u_ref, gain_ref, input_ref, weight_ref, out_ref):
    attn = []
    for h in range(HEADS):
        total = back_ref[h // CORES, h % CORES, 0].astype(jnp.float32)
        for y in range(1, back_ref.shape[2]):
            total += back_ref[h // CORES, h % CORES, y].astype(jnp.float32)
        attn.append(total)
    attn = jnp.concatenate(attn, axis=1) + own_ref[...]
    mean = jnp.mean(attn, axis=1, keepdims=True)
    centered = attn - mean
    var = jnp.mean(centered * centered, axis=1, keepdims=True)
    gate = gain_ref[...] * u_ref[...].astype(jnp.float32)
    normed = (centered * lax.rsqrt(var + eps) * gate).astype(jnp.bfloat16)
    out = jnp.dot(normed, weight_ref[...], preferred_element_type=jnp.float32)
    out_ref[...] = (input_ref[...].astype(jnp.float32) + out).astype(out_ref.dtype)


def finish(back, own, u_act, out_gain, cand_input, out_weight):
    return pl.pallas_call(
        finish_kernel,
        in_specs=[VMEM] * 6,
        out_specs=VMEM,
        out_shape=jax.ShapeDtypeStruct(cand_input.shape, cand_input.dtype),
        compiler_params=pltpu.CompilerParams(vmem_limit_bytes=16 * 1024 * 1024),
        name="finish",
    )(back, own, u_act, out_gain.reshape(1, -1), cand_input, out_weight)


def on_device(
    cand_proj, cand_input, kv_pool, page_owner, page_slot, lengths, block_mask, out_gain, out_weight
):
    rows, width = cand_input.shape
    hd = width // HEADS
    scale = hd ** (-0.5)
    n_z = lax.axis_size("z")
    owners = page_owner.reshape(-1)

    places = page_owner * kv_pool.shape[0] + page_slot
    told = exchange(jnp.broadcast_to(places, (n_z,) + places.shape[1:]), ("z",))
    asked, own, u_act = ask(owners, lengths, block_mask[0].T, cand_proj, scale)
    told, asked = lax.optimization_barrier((told, asked))
    asked = exchange(asked, ("x", "c"))
    pages = split_pages(told.reshape(n_z, -1), kv_pool)
    _, asked = lax.optimization_barrier((pages, asked))
    got = exchange(pages.reshape((-1,) + pages.shape[3:]), PAGES).reshape(pages.shape)
    row, info = asked[:, :rows].reshape(-1, hd), asked[:, rows].astype(jnp.float32)
    part = attend(info, row, got, gather_queries(row), scale)
    back = exchange(part.reshape(-1, rows, hd), SUMS).reshape(part.shape)
    return finish(back, own, u_act, out_gain, cand_input, out_weight)


def solution(mesh):
    n_z, n_p = mesh.shape["batch"], mesh.shape["pos"]
    n_x = HEADS // CORES
    grid = Mesh(mesh.devices.reshape(n_z, n_p // HEADS, n_x, CORES), ("z", "y", "x", "c"))
    rows = P(("z", "y", "x", "c"), None)
    placed = (
        rows,
        rows,
        P("z", None, PLANE, None),
        P("z", PLANE, None),
        P("z", PLANE, None),
        P("z"),
        P("z", None, PLANE),
        P(),
        P(),
    )
    return jax.shard_map(on_device, mesh=grid, in_specs=placed, out_specs=rows, check_vma=False)
```

```python
import functools

import jax
import jax.numpy as jnp
from jax import lax
from jax.experimental import pallas as pl
from jax.experimental.pallas import tpu as pltpu
from jax.sharding import Mesh
from jax.sharding import PartitionSpec as P

HEADS = 8
PAGE = 32
eps = 1e-05

PLANE = ("y", "x", "c")
SPREAD = ("z", "x", "c")
PAGES = ("x", "z", "c")
SUMS = ("x", "c", "y")
CORES = 2

FIELDS = 16
LIVE = 8

LOG2_E = 1.4426950408889634

VMEM = pl.BlockSpec(memory_space=pltpu.VMEM)
SMEM = pl.BlockSpec(memory_space=pltpu.SMEM)
HBM = pl.BlockSpec(memory_space=pl.ANY)


def exchange(array, axes):
    return lax.all_to_all(array, axes, split_axis=0, concat_axis=0, tiled=True)


def shift(array, axis, step):
    n = lax.axis_size(axis)
    return lax.ppermute(array, axis, [(i, (i + step) % n) for i in range(n)])


def silu(value):
    return value / (1.0 + jnp.exp(-value))


def ask_kernel(scale, owner_ref, length_ref, seen_ref, proj_ref, out_ref, own_ref, u_ref):
    pages = owner_ref.shape[0]
    blocks, tiles = seen_ref.shape
    rows, hd = out_ref.shape[1] // 2, out_ref.shape[2]
    place = lax.axis_index(PLANE)
    lane = lax.broadcasted_iota(jnp.int32, (rows, hd), 1)
    owner, field = lane // FIELDS, lane % FIELDS
    seen = []
    for b in range(blocks):
        row = jnp.zeros((rows, hd), jnp.int32)
        for t in range(tiles):
            row = jnp.where(field == t, seen_ref[b : b + 1, t : t + 1], row)
        seen.append(row)
    info = jnp.zeros((rows, hd), jnp.int32)
    for j in range(pages):
        live = jnp.clip(length_ref[0] - (place * pages + j) * PAGE, 0, PAGE)
        row = jnp.where(field == LIVE, live, seen[j * blocks // pages])
        info = jnp.where(owner == owner_ref[j], row, info)
    info = info.astype(jnp.float32).astype(jnp.bfloat16)

    def act(block, h):
        start = (block * HEADS + h) * hd
        return silu(proj_ref[:, start : start + hd].astype(jnp.float32)).astype(jnp.bfloat16)

    for h in range(HEADS):
        part = slice(h * hd, (h + 1) * hd)
        query = act(2, h)
        out_ref[h, :rows] = query
        out_ref[h, rows:] = info
        score = query.astype(jnp.float32) * act(3, h).astype(jnp.float32)
        own = silu(jnp.sum(score, axis=1, keepdims=True) * scale).astype(jnp.bfloat16)
        own_ref[:, part] = own.astype(jnp.float32) * act(1, h).astype(jnp.float32)
        u_ref[:, part] = act(0, h)


def ask(owners, lengths, seen, cand_proj, scale):
    rows, width = cand_proj.shape[0], cand_proj.shape[1] // 4
    hd = width // HEADS
    return pl.pallas_call(
        functools.partial(ask_kernel, scale),
        in_specs=[SMEM] * 2 + [VMEM] * 2,
        out_specs=[VMEM] * 3,
        out_shape=[
            jax.ShapeDtypeStruct((HEADS, 2 * rows, hd), jnp.bfloat16),
            jax.ShapeDtypeStruct((rows, width), jnp.float32),
            jax.ShapeDtypeStruct((rows, width), jnp.bfloat16),
        ],
        name="ask",
    )(owners, lengths, seen, cand_proj)


def split_pages_kernel(told_ref, pool_ref, out_ref, split_ref, sems):
    n_x, users = out_ref.shape[:2]
    hd = out_ref.shape[5]
    count = pool_ref.shape[0]
    first = lax.axis_index("z") * count
    slots = []
    for u in range(users):
        slot = jnp.int32(0)
        for j in range(told_ref.shape[1]):
            at = told_ref[u, j] - first
            slot = jnp.where((at >= 0) & (at < count), at, slot)
        slots.append(slot)
    copies = []
    for u in range(users):
        for k in range(HEADS):
            split_ref[k // CORES, u, k % CORES] = pool_ref[slots[u], :, :, k * hd : (k + 1) * hd]
        copies.append(pltpu.make_async_copy(split_ref.at[:, u], out_ref.at[:, u], sems.at[u]))
        copies[-1].start()
    for copy in copies:
        copy.wait()


def split_pages(told, kv_pool):
    _, _, page, width = kv_pool.shape
    shape = (HEADS // CORES, told.shape[0], CORES, 2, page, width // HEADS)
    return pl.pallas_call(
        split_pages_kernel,
        in_specs=[SMEM, VMEM],
        out_specs=HBM,
        out_shape=jax.ShapeDtypeStruct(shape, kv_pool.dtype),
        scratch_shapes=[pltpu.VMEM(shape, kv_pool.dtype), pltpu.SemaphoreType.DMA((told.shape[0],))],
        name="split_pages",
    )(told, kv_pool)


STEPS = (0, -1, 1, -3, -2, 3, 4, 2)


def gather_queries(row):
    below, above = shift(row, "y", 1), shift(row, "y", -1)
    below3 = shift(jnp.concatenate([row, above]), "y", 3)
    above3 = shift(jnp.concatenate([row, above, below]), "y", -3)
    return below, above, below3, above3


def attend_kernel(scale, info_ref, row_ref, kv_ref, *rest):
    pieces, (out_ref, q_ref, acc_ref) = rest[:-3], rest[-3:]
    n_x, cores, n_y, rows, hd = out_ref.shape
    sources, tiles = n_x * cores, len(STEPS)
    span = sources * PAGE
    height = n_x * cores * rows
    y = lax.axis_index("y")
    blocks = [row_ref[...]]
    for piece in pieces:
        blocks += [piece[b * height : (b + 1) * height, :] for b in range(piece.shape[0] // height)]
    for step, block in zip(STEPS, blocks):
        start = pl.multiple_of(lax.rem(y + (step + tiles), tiles) * height, height)
        q_ref[pl.ds(start, height), :] = block
    place = lax.broadcasted_iota(jnp.int32, (sources, span), 1)
    which = lax.broadcasted_iota(jnp.int32, (sources, span), 0)
    spread = (place // PAGE == which).astype(jnp.bfloat16)
    fields = lax.dot_general(
        info_ref[...].astype(jnp.bfloat16), spread, (((0,), (0,)), ((), ())), preferred_element_type=jnp.float32
    )
    within = lax.rem(lax.broadcasted_iota(jnp.int32, (1, span), 1), PAGE).astype(jnp.float32)
    q = q_ref[...]
    for o in range(kv_ref.shape[1]):
        keys = kv_ref[:, o, :, 0].reshape(span, hd)
        values = kv_ref[:, o, :, 1].reshape(span, hd)
        seen = fields[o * FIELDS : o * FIELDS + tiles]
        live = fields[o * FIELDS + LIVE : o * FIELDS + LIVE + 1]
        allowed = jnp.where(within < live, seen, 0.0).astype(jnp.bfloat16)
        score = lax.dot_general(q, keys, (((1,), (1,)), ((), ())), preferred_element_type=jnp.float32)
        odds = jnp.exp2(score * (-scale * LOG2_E))
        weight = (score * scale / (1.0 + odds)).astype(jnp.bfloat16)
        weight = weight.reshape(tiles, height, span) * allowed[:, None, :]
        part = jnp.dot(weight.reshape(tiles * height, span), values, preferred_element_type=jnp.float32)
        if o == 0:
            acc_ref[...] = part
        else:
            acc_ref[...] += part
    total = acc_ref[...].astype(out_ref.dtype).reshape(n_y, n_x, cores, rows, hd)
    for t in range(n_y):
        out_ref[:, :, t] = total[t]


def attend(info, row, pages, pieces, scale):
    n_x, _, cores, _, _, hd = pages.shape
    rows = row.shape[0] // (n_x * cores)
    out = jax.ShapeDtypeStruct((n_x, cores, len(STEPS), rows, hd), jnp.bfloat16)
    height = out.size // hd
    return pl.pallas_call(
        functools.partial(attend_kernel, scale),
        in_specs=[VMEM] * (3 + len(pieces)),
        out_specs=VMEM,
        out_shape=out,
        scratch_shapes=[pltpu.VMEM((height, hd), jnp.bfloat16), pltpu.VMEM((height, hd), jnp.float32)],
        compiler_params=pltpu.CompilerParams(vmem_limit_bytes=16 * 1024 * 1024),
        name="attend",
    )(info, row, pages, *pieces)


def finish_kernel(back_ref, own_ref, u_ref, gain_ref, input_ref, weight_ref, out_ref):
    attn = []
    for h in range(HEADS):
        total = back_ref[h // CORES, h % CORES, 0].astype(jnp.float32)
        for y in range(1, back_ref.shape[2]):
            total += back_ref[h // CORES, h % CORES, y].astype(jnp.float32)
        attn.append(total)
    attn = jnp.concatenate(attn, axis=1) + own_ref[...]
    mean = jnp.mean(attn, axis=1, keepdims=True)
    centered = attn - mean
    var = jnp.mean(centered * centered, axis=1, keepdims=True)
    gate = gain_ref[...] * u_ref[...].astype(jnp.float32)
    normed = (centered * lax.rsqrt(var + eps) * gate).astype(jnp.bfloat16)
    out = jnp.dot(normed, weight_ref[...], preferred_element_type=jnp.float32)
    out_ref[...] = (input_ref[...].astype(jnp.float32) + out).astype(out_ref.dtype)


def finish(back, own, u_act, out_gain, cand_input, out_weight):
    return pl.pallas_call(
        finish_kernel,
        in_specs=[VMEM] * 6,
        out_specs=VMEM,
        out_shape=jax.ShapeDtypeStruct(cand_input.shape, cand_input.dtype),
        compiler_params=pltpu.CompilerParams(vmem_limit_bytes=16 * 1024 * 1024),
        name="finish",
    )(back, own, u_act, out_gain.reshape(1, -1), cand_input, out_weight)


def on_device(
    cand_proj, cand_input, kv_pool, page_owner, page_slot, lengths, block_mask, out_gain, out_weight
):
    rows, width = cand_input.shape
    hd = width // HEADS
    scale = hd ** (-0.5)
    n_z = lax.axis_size("z")
    owners = page_owner.reshape(-1)

    places = page_owner * kv_pool.shape[0] + page_slot
    told = exchange(jnp.broadcast_to(places, (n_z,) + places.shape[1:]), ("z",))
    asked, own, u_act = ask(owners, lengths, block_mask[0].T, cand_proj, scale)
    told, asked = lax.optimization_barrier((told, asked))
    asked = exchange(asked, ("x", "c"))
    pages = split_pages(told.reshape(n_z, -1), kv_pool)
    _, asked = lax.optimization_barrier((pages, asked))
    got = exchange(pages.reshape((-1,) + pages.shape[3:]), PAGES).reshape(pages.shape)
    row, info = asked[:, :rows].reshape(-1, hd), asked[:, rows].astype(jnp.float32)
    part = attend(info, row, got, gather_queries(row), scale)
    back = exchange(part.reshape(-1, rows, hd), SUMS).reshape(part.shape)
    return finish(back, own, u_act, out_gain, cand_input, out_weight)


def solution(mesh):
    n_z, n_p = mesh.shape["batch"], mesh.shape["pos"]
    n_x = HEADS // CORES
    grid = Mesh(mesh.devices.reshape(n_z, n_p // HEADS, n_x, CORES), ("z", "y", "x", "c"))
    rows = P(("z", "y", "x", "c"), None)
    placed = (
        rows,
        rows,
        P("z", None, PLANE, None),
        P("z", PLANE, None),
        P("z", PLANE, None),
        P("z"),
        P("z", None, PLANE),
        P(),
        P(),
    )
    return jax.shard_map(on_device, mesh=grid, in_specs=placed, out_specs=rows, check_vma=False)
```
